1024 devices in a mesh: gx: 16 (over y_lo, x, core), gz: 64 (over z, y_hi).
Axes of the slice: x: 4, y: 4 (y_hi: 2, y_lo: 2; y = y_hi * 2 + y_lo), z: 32, core: 2. Of those that a mesh axis runs over, the one named last changes fastest.
Arguments:
- conserved: float32 [5, 64, 256, 128], P(None, 'gx', 'gz'), may hold values from -1.1 to 5.5, as said below
- jacobian: float32 [64, 256, 128], P('gx', 'gz'), may hold values from 0.5 to 2
- metric: float32 [3, 3, 64, 256, 128], P(None, None, 'gx', 'gz'), may hold values from -0.45 to 2.01, as said below
- x_master: int32 [32, 64, 32], P('gx', 'gz'), may hold values from 0 to 1, as said below
- x_flip: int32 [32, 64, 32], P('gx', 'gz'), may hold values from 0 to 7, as said below
- z_master: int32 [16, 128, 32], P('gx', 'gz'), may hold values from 0 to 1, as said below
- z_flip: int32 [16, 128, 32], P('gx', 'gz'), may hold values from 0 to 7, as said below
Outputs:
- rhs: float32 [5, 64, 256, 128], P(None, 'gx', 'gz')
The draws below stay inside these ranges and needn't reach their ends.
Inputs may be any that keep to these rules, and one draw needn't show every extreme that they name: conserved[0] is at least 0.6, and the pressure 0.4 (conserved[4] - 0.5 |conserved[1:4]|^2 / conserved[0]) is at least 0.6. metric[g, g] lies between 0.49 and 2.01; every other entry has magnitude at most 0.45. `x_master`: rows 2 t and 2 t + 1 hold the faces on the lower and upper streamwise boundary of tile t; 1 marks that tile t holds the master side. Row 2 t + 1 equals 1 minus row 2 t + 2 (rows taken cyclically), so each face has exactly one master. `x_flip`: rows as in x_master; row 2 t + 1 equals row 2 t + 2 (rows taken cyclically). `z_master`: columns 2 t and 2 t + 1 hold the faces on the lower and upper spanwise boundary of tile t; 1 marks that tile t holds the master side. Column 2 t + 1 equals 1 minus column 2 t + 2 (taken cyclically). `z_flip`: columns as in z_master; column 2 t + 1 equals column 2 t + 2 (taken cyclically).
All inputs are finite; a program needn't handle non-finite values.
Results may differ from the reference program's by a relative error of at most 0.0003.
Values sent between devices are 32-bit elements; how exact they have to be, the bound alone decides.
A program may use at most 64 MiB of HBM per device.

```python
import math
import jax
import jax.numpy as jnp
import numpy as np
from jax import lax

CX = 1
CZ = 1
EY = 32
XTILES = 16
ZTILES = 64
XE = 16
ZE = 64
XN = 64
ZN = 256
YN = 128


def draw_conserved(key, part):
    subkeys = jax.random.split(key, 3)
    grid_dims = (XN, ZN, YN)
    density = jax.random.uniform(subkeys[0], grid_dims, jnp.float32, 0.8, 1.25)
    velocity = 0.3 * jax.random.truncated_normal(subkeys[1], -2.5, 2.5, (3,) + grid_dims, jnp.float32)
    pressure = jax.random.uniform(subkeys[2], grid_dims, jnp.float32, 0.8, 1.25)
    energy = pressure / 0.4 + 0.5 * density * jnp.sum(velocity * velocity, 0)
    return jnp.concatenate([density[None], density[None] * velocity, energy[None]], 0)


def draw_metric(key, part):
    subkeys = jax.random.split(key, 2)
    full_dims = (3, 3, XN, ZN, YN)
    stretch = jnp.exp(jax.random.uniform(subkeys[0], full_dims, jnp.float32, math.log(0.5), math.log(2.0)))
    spread = 0.3
    skew_part = jax.random.uniform(subkeys[1], full_dims, jnp.float32, -spread, spread)
    identity = jnp.eye(3, dtype=jnp.float32).reshape(3, 3, 1, 1, 1)
    return identity * stretch + (1.0 - identity) * skew_part


def draw_x_master(key, part):
    subkeys = jax.random.split(key, 2)
    tile_share = jax.random.randint(subkeys[0], (XTILES, 1, 1), 1, 10)
    vote_draw = jax.random.randint(subkeys[1], (XTILES, ZE, EY), 0, 10)
    lower_flags = (vote_draw < tile_share).astype(jnp.int32)
    upper_flags = 1 - jnp.roll(lower_flags, -1, 0)
    return jnp.stack([lower_flags, upper_flags], 1).reshape(2 * XTILES, ZE, EY)


def draw_x_flip(key, part):
    code_draw = jax.random.randint(key, (XTILES, ZE, EY), 0, 8)
    return jnp.stack([code_draw, jnp.roll(code_draw, -1, 0)], 1).reshape(2 * XTILES, ZE, EY)


def draw_z_master(key, part):
    subkeys = jax.random.split(key, 2)
    tile_share = jax.random.randint(subkeys[0], (1, ZTILES, 1), 1, 10)
    vote_draw = jax.random.randint(subkeys[1], (XE, ZTILES, EY), 0, 10)
    lower_flags = (vote_draw < tile_share).astype(jnp.int32)
    upper_flags = 1 - jnp.roll(lower_flags, -1, 1)
    return jnp.stack([lower_flags, upper_flags], 2).reshape(XE, 2 * ZTILES, EY)


def draw_z_flip(key, part):
    code_draw = jax.random.randint(key, (XE, ZTILES, EY), 0, 8)
    return jnp.stack([code_draw, jnp.roll(code_draw, -1, 1)], 2).reshape(XE, 2 * ZTILES, EY)


def steps_of(stream_key, dims, shards, least, high):
    def one(position, shards_of):
        heights = jax.random.uniform(jax.random.fold_in(jax.random.fold_in(stream_key, 6), position), (shards_of,), jnp.float32, least / len(shards), high / len(shards))
        return jnp.repeat(jnp.exp(heights), dims[position] // shards_of).reshape((-1,) + (1,) * (len(dims) - position - 1))

    factor_of = one(*shards[0])
    for cut in shards[1:]:
        factor_of = factor_of * one(*cut)
    return factor_of


def setup_inputs(seed: int = 0) -> dict:
    keys = jax.random.split(jax.random.key(seed), 8)
    conserved = draw_conserved(jax.random.fold_in(keys[7], 71), 0)
    jacobian = jnp.clip(jnp.exp(math.log(2.0) - 1.3862944 * jax.random.uniform(keys[1], (XN, ZN, YN), jnp.float32) ** steps_of(keys[1], (XN, ZN, YN), ((0, 16), (1, 64)), -0.2, 0.2)), 0.5, 2.0)
    metric = draw_metric(jax.random.fold_in(keys[7], 71), 0)
    x_master = draw_x_master(jax.random.fold_in(keys[7], 71), 0)
    x_flip = draw_x_flip(jax.random.fold_in(keys[7], 71), 0)
    z_master = draw_z_master(jax.random.fold_in(keys[7], 71), 0)
    z_flip = draw_z_flip(jax.random.fold_in(keys[7], 71), 0)
    return dict(conserved=conserved, jacobian=jacobian, metric=metric, x_master=x_master, x_flip=x_flip, z_master=z_master, z_flip=z_flip)


gamma_gas = 1.4
visc_coef = 0.1
prandtl = 0.72
edge_weight = 1.0 / 6.0
highest = lax.Precision.HIGHEST

def node_table():
    points = np.array([-1.0, -math.sqrt(0.2), math.sqrt(0.2), 1.0])
    scales = np.array([np.prod([points[row_index] - points[rest_index] for rest_index in range(4) if rest_index != row_index]) for row_index in range(4)])
    deriv_table = np.zeros((4, 4))
    for row_index in range(4):
        for col_index in range(4):
            if row_index != col_index:
                deriv_table[row_index, col_index] = scales[row_index] / (scales[col_index] * (points[row_index] - points[col_index]))
        deriv_table[row_index, row_index] = -np.sum(deriv_table[row_index])
    return deriv_table

def derive(values, axis_pos):
    moved_last = jnp.moveaxis(values, axis_pos, -1)
    length = moved_last.shape[-1]
    grouped = moved_last.reshape(moved_last.shape[:-1] + (length // 4, 4))
    result = jnp.einsum('...n,mn->...m', grouped, jnp.asarray(node_table(), jnp.float32), precision=highest)
    return jnp.moveaxis(result.reshape(moved_last.shape), -1, axis_pos)

def primitives(values):
    density = values[0]
    velocity = values[1:4] / density
    pressure = (gamma_gas - 1.0) * (values[4] - 0.5 * density * lax.optimization_barrier(jnp.sum(velocity * velocity, 0)))
    return (density, velocity, pressure)

def lifted_of(values):
    density, velocity, pressure = primitives(values)
    return jnp.concatenate([velocity, (pressure / density)[None]], 0)

def total_flux(values, gradient):
    density, velocity, pressure = primitives(values)
    slopes = gradient.reshape((4, 3) + gradient.shape[1:])
    divergence = slopes[0, 0] + slopes[1, 1] + slopes[2, 2]
    heat_coef = visc_coef * gamma_gas / ((gamma_gas - 1.0) * prandtl)
    directions = []
    for direction in range(3):
        stress = [visc_coef * (slopes[component, direction] + slopes[direction, component]) for component in range(3)]
        stress[direction] = stress[direction] - 2.0 / 3.0 * visc_coef * divergence
        moment = [values[1 + component] * velocity[direction] - stress[component] for component in range(3)]
        moment[direction] = moment[direction] + pressure
        viscous_work = velocity[0] * stress[0] + velocity[1] * stress[1] + velocity[2] * stress[2]
        energy_flux = (values[4] + pressure) * velocity[direction] - viscous_work - heat_coef * slopes[3, direction]
        directions.append(jnp.stack([values[1 + direction]] + moment + [energy_flux]))
    return jnp.stack(directions)

def normal_part(flux, normal):
    return flux[0] * normal[0] + flux[1] * normal[1] + flux[2] * normal[2]

def wave_bound(values, normal):
    density, velocity, pressure = primitives(values)
    normal_size = jnp.sqrt(lax.optimization_barrier(jnp.sum(normal * normal, 0)))
    return jnp.abs(lax.optimization_barrier(jnp.sum(velocity * normal, 0))) + jnp.sqrt(gamma_gas * pressure / density) * normal_size

def mirror(values):
    return jnp.concatenate([values[0:1], -values[1:4], values[4:]], 0)

def take_range(values, start_at, stop_at, axis_pos):
    return lax.slice_in_dim(values, start_at, stop_at, 1, axis_pos)

def face_layers(values, axis_pos):
    length = values.shape[axis_pos]
    lowers = lax.slice_in_dim(values, 0, length, 4, axis_pos)
    uppers = lax.slice_in_dim(values, 3, length, 4, axis_pos)
    return (lowers, uppers)

def place_faces(lowers, uppers, axis_pos):
    middle = jnp.zeros_like(lowers)
    stacked = jnp.stack([lowers, middle, middle, uppers], axis_pos + 1)
    merged_dims = list(lowers.shape)
    merged_dims[axis_pos] = merged_dims[axis_pos] * 4
    return stacked.reshape(merged_dims)

def orient(layer_in, code_in, axis_pos, inverse):
    fields = layer_in.shape[0]
    if axis_pos == 1:
        blocks = layer_in.reshape(fields, layer_in.shape[1], layer_in.shape[2] // 4, 4, layer_in.shape[3] // 4, 4)
        code_grid = code_in[None, :, :, None, :, None]
        axis_one, axis_two = (3, 5)
    else:
        blocks = layer_in.reshape(fields, layer_in.shape[1] // 4, 4, layer_in.shape[2], layer_in.shape[3] // 4, 4)
        code_grid = code_in[None, :, None, :, :, None]
        axis_one, axis_two = (2, 5)
    swap_bit = code_grid // 4 % 2 == 1
    first_bit = code_grid % 2 == 1
    second_bit = code_grid // 2 % 2 == 1
    if inverse:
        blocks = jnp.where(second_bit, jnp.flip(blocks, axis_two), blocks)
        blocks = jnp.where(first_bit, jnp.flip(blocks, axis_one), blocks)
        blocks = jnp.where(swap_bit, jnp.swapaxes(blocks, axis_one, axis_two), blocks)
    else:
        blocks = jnp.where(swap_bit, jnp.swapaxes(blocks, axis_one, axis_two), blocks)
        blocks = jnp.where(first_bit, jnp.flip(blocks, axis_one), blocks)
        blocks = jnp.where(second_bit, jnp.flip(blocks, axis_two), blocks)
    return blocks.reshape(layer_in.shape)

def node_mask(flags, axis_pos):
    if axis_pos == 1:
        return jnp.repeat(jnp.repeat(flags, 4, 1), 4, 2)
    return jnp.repeat(jnp.repeat(flags, 4, 0), 4, 2)

def edge_tables(masters, flip_codes, per_tile, tile_axis):
    tile_total = masters.shape[tile_axis] // 2
    lower_masters = lax.slice_in_dim(masters, 0, 2 * tile_total, 2, tile_axis)
    lower_flips = lax.slice_in_dim(flip_codes, 0, 2 * tile_total, 2, tile_axis)
    element_total = tile_total * per_tile
    element = jnp.arange(element_total)
    up_tile = (element + 1) // per_tile % tile_total
    low_tile = element // per_tile
    mask_dims = [1, 1, 1]
    mask_dims[tile_axis] = element_total
    up_edge = ((element + 1) % per_tile == 0).reshape(mask_dims)
    low_edge = (element % per_tile == 0).reshape(mask_dims)
    up_flag = jnp.take(lower_masters, up_tile, axis=tile_axis)
    low_flag = jnp.take(lower_masters, low_tile, axis=tile_axis)
    up_lead = jnp.logical_not(up_edge) | (up_flag == 0)
    low_lead = jnp.logical_not(low_edge) | (low_flag == 0)
    up_code = jnp.where(up_edge, jnp.take(lower_flips, up_tile, axis=tile_axis), 0)
    low_code = jnp.where(low_edge, jnp.take(lower_flips, low_tile, axis=tile_axis), 0)
    return (up_lead, up_code, low_lead, low_code)

def wall_record(conserved, metric):
    stacked = jnp.concatenate([conserved, metric[2]], 0)
    lowers, uppers = face_layers(stacked, 3)
    element_total = lowers.shape[3]
    partner_up = jnp.concatenate([take_range(lowers, 1, element_total, 3), mirror(take_range(uppers, element_total - 1, element_total, 3))], 3)
    partner_low = jnp.concatenate([mirror(take_range(lowers, 0, 1, 3)), take_range(uppers, 0, element_total - 1, 3)], 3)
    return (3, lowers, uppers, partner_low, partner_up, partner_low[5:8], uppers[5:8])

def lift_surface(own_values, other_values, normal, own_metric, side_sign):
    average = 0.5 * (own_values + other_values)
    terms = average[:, None] * normal[None] - own_values[:, None] * own_metric[None]
    return side_sign / edge_weight * terms.reshape((12,) + own_values.shape[1:])

def lift_all(records, lifted, metric, jacobian):
    gradient_sum = 0.0
    for record in records:
        axis_pos, lowers, uppers, partner_low, partner_up, normal_low, normal_up = record[:7]
        metric_rows = metric[axis_pos - 1]
        volume_terms = (lifted[:, None] * metric_rows[None]).reshape((12,) + lifted.shape[1:])
        surf_low = lift_surface(lifted_of(lowers[:5]), lifted_of(partner_low[:5]), normal_low, lowers[5:8], -1.0)
        surf_up = lift_surface(lifted_of(uppers[:5]), lifted_of(partner_up[:5]), normal_up, uppers[5:8], 1.0)
        gradient_sum = gradient_sum + derive(volume_terms, axis_pos) + place_faces(surf_low, surf_up, axis_pos)
    return gradient_sum / jacobian

def face_terms(own_state, other_state, own_half, other_half, normal, own_contra, upper_side):
    fastest = jnp.maximum(wave_bound(own_state, normal), wave_bound(other_state, normal))
    if upper_side:
        state_jump = other_state - own_state
        side_sign = 1.0
    else:
        state_jump = own_state - other_state
        side_sign = -1.0
    face_flux = 0.5 * (own_half + other_half) - 0.5 * fastest * state_jump
    return side_sign / edge_weight * (face_flux - own_contra)

def face_section(record, own_pair, other_pair, contra):
    axis_pos, lowers, uppers, partner_low, partner_up, normal_low, normal_up = record[:7]
    contra_low, contra_up = face_layers(contra, axis_pos)
    terms_low = face_terms(lowers[:5], partner_low[:5], own_pair[0], other_pair[0], normal_low, contra_low, False)
    terms_up = face_terms(uppers[:5], partner_up[:5], own_pair[1], other_pair[1], normal_up, contra_up, True)
    return derive(contra, axis_pos) + place_faces(terms_low, terms_up, axis_pos)

def reference(conserved, jacobian, metric, x_master, x_flip, z_master, z_flip):
    lifted = lifted_of(conserved)
    records = []
    for axis_pos, masters, flip_codes, per_tile in ((1, x_master, x_flip, CX), (2, z_master, z_flip, CZ)):
        up_lead, up_code, low_lead, low_code = edge_tables(masters, flip_codes, per_tile, axis_pos - 1)
        stacked = jnp.concatenate([conserved, metric[axis_pos - 1]], 0)
        lowers, uppers = face_layers(stacked, axis_pos)
        partner_up = orient(jnp.roll(lowers, -1, axis_pos), up_code, axis_pos, False)
        partner_low = orient(jnp.roll(uppers, 1, axis_pos), low_code, axis_pos, True)
        normal_up = jnp.where(node_mask(up_lead, axis_pos), uppers[5:8], partner_up[5:8])
        normal_low = jnp.where(node_mask(low_lead, axis_pos), partner_low[5:8], lowers[5:8])
        records.append((axis_pos, lowers, uppers, partner_low, partner_up, normal_low, normal_up, up_code, low_code))
    records.append(wall_record(conserved, metric))
    gradient = lift_all(records, lifted, metric, jacobian)
    volume_flux = total_flux(conserved, gradient)
    rhs_sum = 0.0
    for record in records:
        axis_pos, lowers, uppers, partner_low, partner_up, normal_low, normal_up = record[:7]
        grad_low, grad_up = face_layers(gradient, axis_pos)
        if axis_pos == 3:
            element_total = grad_low.shape[3]
            other_grad_low = jnp.concatenate([take_range(grad_low, 0, 1, 3), take_range(grad_up, 0, element_total - 1, 3)], 3)
            other_grad_up = jnp.concatenate([take_range(grad_low, 1, element_total, 3), take_range(grad_up, element_total - 1, element_total, 3)], 3)
        else:
            other_grad_up = orient(jnp.roll(grad_low, -1, axis_pos), record[7], axis_pos, False)
            other_grad_low = orient(jnp.roll(grad_up, 1, axis_pos), record[8], axis_pos, True)
        own_pair = (normal_part(total_flux(lowers[:5], grad_low), normal_low), normal_part(total_flux(uppers[:5], grad_up), normal_up))
        other_pair = (normal_part(total_flux(partner_low[:5], other_grad_low), normal_low), normal_part(total_flux(partner_up[:5], other_grad_up), normal_up))
        contra = normal_part(volume_flux, metric[axis_pos - 1])
        rhs_sum = rhs_sum + face_section(record, own_pair, other_pair, contra)
    return -rhs_sum / jacobian
```

```python
import functools
import math

import jax
import jax.numpy as jnp
import numpy as np
from jax import lax
from jax.experimental import pallas as pl
from jax.experimental.pallas import tpu as pltpu
from jax.sharding import PartitionSpec as P

MESH = pl.DeviceIdType.MESH
gamma_gas = 1.4
visc_coef = 0.1
prandtl = 0.72
heat_ratio = gamma_gas / ((gamma_gas - 1.0) * prandtl)


def node_table():
    points = np.array([-1.0, -math.sqrt(0.2), math.sqrt(0.2), 1.0])
    scales = np.array(
        [np.prod([points[r] - points[s] for s in range(4) if s != r]) for r in range(4)]
    )
    table = np.zeros((4, 4))
    for r in range(4):
        for c in range(4):
            if r != c:
                table[r, c] = scales[r] / (scales[c] * (points[r] - points[c]))
        table[r, r] = -np.sum(table[r])
    return table


weak = node_table()
weak[0, 0] += 6.0
weak[3, 3] -= 6.0


def pick(index, values):
    result = jnp.full(index.shape, float(values[3]), jnp.float32)
    for at in range(3):
        result = jnp.where(index == at, float(values[at]), result)
    return result


def along(values, index, axis):
    shape = values.shape
    flat = values.reshape((-1, 8, 128))
    parts = [
        jnp.take_along_axis(flat[n], index, axis=axis, mode="promise_in_bounds")
        for n in range(flat.shape[0])
    ]
    return jnp.stack(parts).reshape(shape)


def primitives(state):
    inverse = 1.0 / state[0]
    velocity = [state[1 + j] * inverse for j in range(3)]
    kinetic = state[1] * velocity[0] + state[2] * velocity[1] + state[3] * velocity[2]
    pressure = (gamma_gas - 1.0) * (state[4] - 0.5 * kinetic)
    return velocity, pressure, pressure * inverse


def dot3(left, right):
    return left[0] * right[0] + left[1] * right[1] + left[2] * right[2]


def fluxes(state, velocity, pressure, slopes):
    third = (2.0 / 3.0) * (slopes[0][0] + slopes[1][1] + slopes[2][2])
    stress = [[None] * 3 for _ in range(3)]
    moment = [[None] * 3 for _ in range(3)]
    for j in range(3):
        for d in range(j, 3):
            tau = slopes[j][d] + slopes[d][j]
            flow = state[1 + j] * velocity[d]
            if j == d:
                tau = tau - third
                flow = flow + pressure
            stress[j][d] = stress[d][j] = tau
            moment[j][d] = moment[d][j] = flow - tau
    total = state[4] + pressure
    energy = [
        total * velocity[d] - dot3(velocity, stress[d]) - heat_ratio * slopes[3][d]
        for d in range(3)
    ]
    return moment, energy


def wave(velocity, sound, normal, size):
    return jnp.abs(dot3(velocity, normal)) + sound * size


def kernel(
    nx, nz, cons_n, met_n, jac_n, cons_f, met_f, xm, xf, zm, zf, out,
    nodes, metv, jacv, face, recv1, send2, recv2, codes, lsem, csem, s1, r1, s2, r2,
):
    gx, gz = lax.axis_index("gx"), lax.axis_index("gz")
    x_up, x_low = lax.rem(gx + 1, nx), lax.rem(gx + nx - 1, nx)
    z_up, z_low = lax.rem(gz + 1, nz), lax.rem(gz + nz - 1, nz)
    targets = [(x_up, gz), (x_low, gz), (gx, z_up), (gx, z_low)]

    barrier = pltpu.get_barrier_semaphore()
    for target in targets:
        pl.semaphore_signal(barrier, inc=1, device_id=target, device_id_type=MESH)

    low, up = pl.ds(0, 4), pl.ds(4, 4)
    five, three = pl.ds(0, 5), pl.ds(5, 3)
    packs = [
        (cons_f.at[:, 0], face.at[0, five, low]),
        (cons_f.at[:, 3], face.at[0, five, up]),
        (met_f.at[0, :, 0], face.at[0, three, low]),
        (met_f.at[0, :, 3], face.at[0, three, up]),
        (cons_f.at[:, :, 0, :], face.at[1, five, low]),
        (cons_f.at[:, :, 3, :], face.at[1, five, up]),
        (met_f.at[1, :, :, 0, :], face.at[1, three, low]),
        (met_f.at[1, :, :, 3, :], face.at[1, three, up]),
    ]
    packs = [pltpu.make_async_copy(a, b, lsem.at[n]) for n, (a, b) in enumerate(packs)]
    loads = [(cons_n, nodes), (met_n, metv), (jac_n, jacv)]
    loads += [(ref, codes.at[n]) for n, ref in enumerate((xm, xf, zm, zf))]
    loads = [pltpu.make_async_copy(a, b, csem.at[n]) for n, (a, b) in enumerate(loads)]
    for copy in packs + loads:
        copy.start()

    sub = lax.broadcasted_iota(jnp.int32, (8, 128), 0)
    lane = lax.broadcasted_iota(jnp.int32, (8, 128), 1)
    row, col = sub & 3, lane & 3
    lower = sub < 4
    half = sub >> 2
    side = jnp.where(lower, -1.0, 1.0)
    x_node = [jnp.where(lower, 1.0, 0.0), jnp.where(lower, 0.0, 1.0)]
    z_edge = jnp.where((row == 0) | (row == 3), 1.0, 0.0)
    cross_index = half * 3 + jnp.where(row == 3, 4, 0)
    z_index = half + jnp.where(row == 3, 4, 0)
    z_from = ((sub & 1) << 2) + half * 3
    z_first = row < 2
    cz = [pick(row, [weak[a, a ^ s] for a in range(4)]) for s in range(4)]
    cy = [pick(col, [weak[a, a ^ s] for a in range(4)]) for s in range(4)]
    cx = [
        [
            [
                jnp.where(lower, float(weak[2 * v, 2 * w + s]), float(weak[2 * v + 1, 2 * w + 1 - s]))
                for s in range(2)
            ]
            for w in range(2)
        ]
        for v in range(2)
    ]
    wall = (lane == 0) | (lane == 127)
    wall_sign = jnp.where(wall, -1.0, 1.0)
    y_other = jnp.where(
        wall, lane, jnp.where(col == 0, lane - 1, jnp.where(col == 3, lane + 1, lane))
    )
    y_lead = jnp.where((col == 0) & (lane > 0), lane - 1, lane)
    y_side = jnp.where(col == 0, -3.0, jnp.where(col == 3, 3.0, 0.0))
    y_jump = jnp.abs(y_side)

    def d_x(v):
        r = jnp.stack([pltpu.roll(v[n], 4, 1) for n in range(v.shape[0])])
        parts = [
            cx[n][0][0] * v[:, 0] + cx[n][0][1] * r[:, 0] + cx[n][1][0] * v[:, 1] + cx[n][1][1] * r[:, 1]
            for n in range(2)
        ]
        return jnp.stack(parts, 1)

    def d_z(v):
        result = cz[0] * v
        for s in range(1, 4):
            result = result + cz[s] * along(v, sub ^ s, 0)
        return result

    def d_y(v):
        result = cy[0] * v
        for s in range(1, 4):
            result = result + cy[s] * along(v, lane ^ s, 1)
        return result

    def to_faces(v):
        ends = along(v, z_from, 0)
        return jnp.stack([jnp.where(lower, v[0], v[1]), jnp.where(z_first, ends[0], ends[1])])

    def to_nodes(f):
        z0 = along(f[1], z_index, 0)
        z1 = along(f[1], z_index + 2, 0)
        return jnp.stack([f[0] * x_node[0] + z0 * z_edge, f[0] * x_node[1] + z1 * z_edge])

    for copy in packs:
        copy.wait()
    pl.semaphore_wait(barrier, 4)
    sends1 = []
    for n, target in enumerate(targets):
        axis, from_up = n // 2, n % 2 == 0
        sends1.append(
            pltpu.make_async_remote_copy(
                src_ref=face.at[axis, :, up if from_up else low],
                dst_ref=recv1.at[axis, :, low if from_up else up],
                send_sem=s1.at[n],
                recv_sem=r1.at[n],
                device_id=target,
                device_id_type=MESH,
            )
        )
    for copy in sends1:
        copy.start()

    for copy in loads:
        copy.wait()
    lead, lane_one, row_two, lane_three = [], [], [], []
    for axis in range(2):
        word = codes[2 * axis + 1] + 8 * codes[2 * axis]
        word = jnp.where(
            lax.broadcasted_iota(jnp.int32, (8, 32), 0) < 4,
            jnp.broadcast_to(word[0:1], (8, 32)),
            jnp.broadcast_to(word[1:2], (8, 32)),
        )
        word = along(jnp.concatenate([word] * 4, 1), lane >> 2, 1)
        first, second = (word & 1) * 3, ((word >> 1) & 1) * 3
        swap = (word & 4) != 0
        lead.append((word & 8) != 0)
        lane_one.append(lane ^ jnp.where(swap, row ^ first ^ second, second))
        row_two.append(
            sub ^ jnp.where(swap, col ^ jnp.where(lower, first, second), first)
        )
        lane_three.append(lane ^ jnp.where(swap, row, 0))

    def orient(axis, layer):
        layer = along(layer, lane_one[axis], 1)
        layer = along(layer, row_two[axis], 0)
        return along(layer, lane_three[axis], 1)

    state = [nodes[k] for k in range(5)]
    metric = [[metv[g, d] for d in range(3)] for g in range(3)]
    velocity, pressure, warm = primitives(state)
    lifted = jnp.stack(velocity + [warm])
    inverse_j = 1.0 / jacv[...]

    def products(g):
        return (lifted[:, None] * jnp.stack(metric[g])[None]).reshape(12, 2, 8, 128)

    partial = d_x(products(0)) + d_z(products(1)) + d_y(products(2))
    y_normal = [along(metric[2][d], y_lead, 1) for d in range(3)]
    y_sums = [
        y_side * (lifted[k] + (wall_sign if k < 3 else 1.0) * along(lifted[k], y_other, 1))
        for k in range(4)
    ]
    partial = [
        [partial[3 * k + d] + y_sums[k] * y_normal[d] for d in range(3)] for k in range(4)
    ]
    scaled = visc_coef * inverse_j
    face_partial = [[to_faces(partial[k][d]) for d in range(3)] for k in range(4)]
    face_scaled = to_faces(scaled)
    own = [face[:, k] for k in range(8)]
    own_velocity, own_pressure, own_warm = primitives(own)
    own_lifted = own_velocity + [own_warm]

    for copy in sends1:
        copy.wait_recv()
    other = [
        jnp.stack([orient(axis, recv1[axis, k]) for axis in range(2)]) for k in range(8)
    ]
    leads = jnp.stack(lead)
    normal = [jnp.where(leads, own[5 + d], other[5 + d]) for d in range(3)]
    other_velocity, other_pressure, other_warm = primitives(other)
    other_lifted = other_velocity + [other_warm]
    sums = [(3.0 * side) * (own_lifted[k] + other_lifted[k]) for k in range(4)]

    def crossed(f):
        return jnp.stack([along(f[1], cross_index, 0), along(f[0], cross_index, 0)])

    cross_sums = [z_edge * crossed(sums[k]) for k in range(4)]
    cross_normal = [crossed(normal[d]) for d in range(3)]
    face_slopes = [
        [
            face_scaled
            * (face_partial[k][d] + sums[k] * normal[d] + cross_sums[k] * cross_normal[d])
            for d in range(3)
        ]
        for k in range(4)
    ]
    moment, energy = fluxes(own, own_velocity, own_pressure, face_slopes)
    own_half = [dot3(moment[j], normal) for j in range(3)] + [dot3(energy, normal)]
    for k in range(4):
        send2[:, k] = own_half[k]

    sends2 = []
    for n, target in enumerate(targets):
        axis, from_up = n // 2, n % 2 == 0
        sends2.append(
            pltpu.make_async_remote_copy(
                src_ref=send2.at[axis, :, up if from_up else low],
                dst_ref=recv2.at[axis, :, low if from_up else up],
                send_sem=s2.at[n],
                recv_sem=r2.at[n],
                device_id=target,
                device_id_type=MESH,
            )
        )
    for copy in sends2:
        copy.start()

    z_sums = [jnp.stack([along(sums[k][1], z_index, 0), along(sums[k][1], z_index + 2, 0)]) * z_edge for k in range(4)]
    z_normal = [jnp.stack([along(normal[d][1], z_index, 0), along(normal[d][1], z_index + 2, 0)]) for d in range(3)]
    x_mask = jnp.stack(x_node)
    slopes = [
        [
            scaled
            * (
                partial[k][d]
                + x_mask * (sums[k][0] * normal[d][0])
                + z_sums[k] * z_normal[d]
            )
            for d in range(3)
        ]
        for k in range(4)
    ]
    moment, energy = fluxes(state, velocity, pressure, slopes)

    def through(rows):
        parts = [dot3(state[1:4], rows)]
        parts += [dot3(moment[j], rows) for j in range(3)]
        return parts + [dot3(energy, rows)]

    total = d_x(jnp.stack(through(metric[0])))
    total = total + d_z(jnp.stack(through(metric[1])))
    total = total + d_y(jnp.stack(through(metric[2])))

    half_y = through(y_normal)
    heat_y = (-2.0 * heat_ratio) * dot3(slopes[3], y_normal)
    size_y = jnp.sqrt(dot3(y_normal, y_normal))
    speed = wave(velocity, jnp.sqrt(gamma_gas * warm), y_normal, size_y)
    speed = y_jump * jnp.maximum(speed, along(speed, y_other, 1))
    y_terms = []
    for k in range(5):
        sign = wall_sign if 1 <= k <= 3 else 1.0
        jump = sign * along(state[k], y_other, 1) - state[k]
        sign = wall_sign if k == 0 else 1.0
        both = half_y[k] + sign * along(half_y[k], y_other, 1)
        if k == 4:
            both = jnp.where(wall, heat_y, both)
        y_terms.append(y_side * both - speed * jump)

    size = jnp.sqrt(dot3(normal, normal))
    speed = jnp.maximum(
        wave(own_velocity, jnp.sqrt(gamma_gas * own_warm), normal, size),
        wave(other_velocity, jnp.sqrt(gamma_gas * other_warm), normal, size),
    )
    known = [dot3([own[1 + d] + other[1 + d] for d in range(3)], normal)] + own_half
    known = [
        (3.0 * side) * known[k] - (3.0 * speed) * (other[k] - own[k]) for k in range(5)
    ]
    out[0] = -inverse_j * (total[0] + y_terms[0] + to_nodes(known[0]))
    rest = [total[k] + y_terms[k] + to_nodes(known[k]) for k in range(1, 5)]

    for copy in sends2:
        copy.wait_recv()
    for k in range(4):
        arrived = jnp.stack([orient(axis, recv2[axis, k]) for axis in range(2)])
        out[1 + k] = -inverse_j * (rest[k] + to_nodes((3.0 * side) * arrived))
    for copy in sends1 + sends2:
        copy.wait_send()


def local(nx, nz, conserved, jacobian, metric, x_master, x_flip, z_master, z_flip):
    anywhere = pl.BlockSpec(memory_space=pl.ANY)
    words = [v.reshape(2, 32) for v in (x_master, x_flip, z_master, z_flip)]
    result = pl.pallas_call(
        functools.partial(kernel, nx, nz),
        out_shape=jax.ShapeDtypeStruct((5, 2, 8, 128), jnp.float32),
        in_specs=[anywhere] * 9,
        out_specs=pl.BlockSpec(memory_space=pltpu.VMEM),
        scratch_shapes=[
            pltpu.VMEM((5, 2, 8, 128), jnp.float32),
            pltpu.VMEM((3, 3, 2, 8, 128), jnp.float32),
            pltpu.VMEM((2, 8, 128), jnp.float32),
            pltpu.VMEM((2, 8, 8, 128), jnp.float32),
            pltpu.VMEM((2, 8, 8, 128), jnp.float32),
            pltpu.VMEM((2, 4, 8, 128), jnp.float32),
            pltpu.VMEM((2, 4, 8, 128), jnp.float32),
            pltpu.VMEM((4, 2, 32), jnp.int32),
            pltpu.SemaphoreType.DMA((8,)),
            pltpu.SemaphoreType.DMA((7,)),
            pltpu.SemaphoreType.DMA((4,)),
            pltpu.SemaphoreType.DMA((4,)),
            pltpu.SemaphoreType.DMA((4,)),
            pltpu.SemaphoreType.DMA((4,)),
        ],
        compiler_params=pltpu.CompilerParams(collective_id=0, has_side_effects=True),
    )(
        conserved.reshape(5, 2, 8, 128),
        metric.reshape(3, 3, 2, 8, 128),
        jacobian.reshape(2, 8, 128),
        conserved,
        metric,
        *words,
    )
    return result.reshape(5, 4, 4, 128)


def solution(mesh):
    flags = P("gx", "gz", None)
    in_specs = (P(None, "gx", "gz", None), flags, P(None, None, "gx", "gz", None)) + (flags,) * 4
    return jax.shard_map(
        functools.partial(local, mesh.shape["gx"], mesh.shape["gz"]),
        mesh=mesh,
        in_specs=in_specs,
        out_specs=P(None, "gx", "gz", None),
        check_vma=False,
    )
```

```python
import functools
import math

import jax
import jax.numpy as jnp
import numpy as np
from jax import lax
from jax.experimental import pallas as pl
from jax.experimental.pallas import tpu as pltpu
from jax.sharding import PartitionSpec as P

MESH = pl.DeviceIdType.MESH
gamma_gas = 1.4
visc_coef = 0.1
prandtl = 0.72
heat_ratio = gamma_gas / ((gamma_gas - 1.0) * prandtl)


def node_table():
    points = np.array([-1.0, -math.sqrt(0.2), math.sqrt(0.2), 1.0])
    scales = np.array(
        [np.prod([points[r] - points[s] for s in range(4) if s != r]) for r in range(4)]
    )
    table = np.zeros((4, 4))
    for r in range(4):
        for c in range(4):
            if r != c:
                table[r, c] = scales[r] / (scales[c] * (points[r] - points[c]))
        table[r, r] = -np.sum(table[r])
    return table


weak = node_table()
weak[0, 0] += 6.0
weak[3, 3] -= 6.0


def pick(index, values):
    result = jnp.full(index.shape, float(values[3]), jnp.float32)
    for at in range(3):
        result = jnp.where(index == at, float(values[at]), result)
    return result


def along(values, index, axis):
    shape = values.shape
    flat = values.reshape((-1, 8, 128))
    parts = [
        jnp.take_along_axis(flat[n], index, axis=axis, mode="promise_in_bounds")
        for n in range(flat.shape[0])
    ]
    return jnp.stack(parts).reshape(shape)


def primitives(state):
    inverse = 1.0 / state[0]
    velocity = [state[1 + j] * inverse for j in range(3)]
    kinetic = state[1] * velocity[0] + state[2] * velocity[1] + state[3] * velocity[2]
    pressure = (gamma_gas - 1.0) * (state[4] - 0.5 * kinetic)
    return velocity, pressure, pressure * inverse


def dot3(left, right):
    return left[0] * right[0] + left[1] * right[1] + left[2] * right[2]


def fluxes(state, velocity, pressure, slopes):
    third = (2.0 / 3.0) * (slopes[0][0] + slopes[1][1] + slopes[2][2])
    stress = [[None] * 3 for _ in range(3)]
    moment = [[None] * 3 for _ in range(3)]
    for j in range(3):
        for d in range(j, 3):
            tau = slopes[j][d] + slopes[d][j]
            flow = state[1 + j] * velocity[d]
            if j == d:
                tau = tau - third
                flow = flow + pressure
            stress[j][d] = stress[d][j] = tau
            moment[j][d] = moment[d][j] = flow - tau
    total = state[4] + pressure
    energy = [
        total * velocity[d] - dot3(velocity, stress[d]) - heat_ratio * slopes[3][d]
        for d in range(3)
    ]
    return moment, energy


def wave(velocity, sound, normal, size):
    return jnp.abs(dot3(velocity, normal)) + sound * size


def kernel(
    nx, nz, cons_n, met_n, jac_n, cons_f, met_f, xm, xf, zm, zf, out,
    nodes, metv, jacv, face, recv1, send2, recv2, codes, lsem, csem, s1, r1, s2, r2,
):
    gx, gz = lax.axis_index("gx"), lax.axis_index("gz")
    x_up, x_low = lax.rem(gx + 1, nx), lax.rem(gx + nx - 1, nx)
    z_up, z_low = lax.rem(gz + 1, nz), lax.rem(gz + nz - 1, nz)
    targets = [(x_up, gz), (x_low, gz), (gx, z_up), (gx, z_low)]

    barrier = pltpu.get_barrier_semaphore()
    for target in targets:
        pl.semaphore_signal(barrier, inc=1, device_id=target, device_id_type=MESH)

    low, up = pl.ds(0, 4), pl.ds(4, 4)
    five, three = pl.ds(0, 5), pl.ds(5, 3)
    packs = [
        (cons_f.at[:, 0], face.at[0, five, low]),
        (cons_f.at[:, 3], face.at[0, five, up]),
        (met_f.at[0, :, 0], face.at[0, three, low]),
        (met_f.at[0, :, 3], face.at[0, three, up]),
        (cons_f.at[:, :, 0, :], face.at[1, five, low]),
        (cons_f.at[:, :, 3, :], face.at[1, five, up]),
        (met_f.at[1, :, :, 0, :], face.at[1, three, low]),
        (met_f.at[1, :, :, 3, :], face.at[1, three, up]),
    ]
    packs = [pltpu.make_async_copy(a, b, lsem.at[n]) for n, (a, b) in enumerate(packs)]
    loads = [(cons_n, nodes), (met_n, metv), (jac_n, jacv)]
    loads += [(ref, codes.at[n]) for n, ref in enumerate((xm, xf, zm, zf))]
    loads = [pltpu.make_async_copy(a, b, csem.at[n]) for n, (a, b) in enumerate(loads)]
    for copy in packs + loads:
        copy.start()

    sub = lax.broadcasted_iota(jnp.int32, (8, 128), 0)
    lane = lax.broadcasted_iota(jnp.int32, (8, 128), 1)
    row, col = sub & 3, lane & 3
    lower = sub < 4
    half = sub >> 2
    side = jnp.where(lower, -1.0, 1.0)
    x_node = [jnp.where(lower, 1.0, 0.0), jnp.where(lower, 0.0, 1.0)]
    z_edge = jnp.where((row == 0) | (row == 3), 1.0, 0.0)
    cross_index = half * 3 + jnp.where(row == 3, 4, 0)
    z_index = half + jnp.where(row == 3, 4, 0)
    z_from = ((sub & 1) << 2) + half * 3
    z_first = row < 2
    cz = [pick(row, [weak[a, a ^ s] for a in range(4)]) for s in range(4)]
    cy = [pick(col, [weak[a, a ^ s] for a in range(4)]) for s in range(4)]
    cx = [
        [
            [
                jnp.where(lower, float(weak[2 * v, 2 * w + s]), float(weak[2 * v + 1, 2 * w + 1 - s]))
                for s in range(2)
            ]
            for w in range(2)
        ]
        for v in range(2)
    ]
    wall = (lane == 0) | (lane == 127)
    wall_sign = jnp.where(wall, -1.0, 1.0)
    y_other = jnp.where(
        wall, lane, jnp.where(col == 0, lane - 1, jnp.where(col == 3, lane + 1, lane))
    )
    y_lead = jnp.where((col == 0) & (lane > 0), lane - 1, lane)
    y_side = jnp.where(col == 0, -3.0, jnp.where(col == 3, 3.0, 0.0))
    y_jump = jnp.abs(y_side)

    def d_x(v):
        r = jnp.stack([pltpu.roll(v[n], 4, 1) for n in range(v.shape[0])])
        parts = [
            cx[n][0][0] * v[:, 0] + cx[n][0][1] * r[:, 0] + cx[n][1][0] * v[:, 1] + cx[n][1][1] * r[:, 1]
            for n in range(2)
        ]
        return jnp.stack(parts, 1)

    def d_z(v):
        result = cz[0] * v
        for s in range(1, 4):
            result = result + cz[s] * along(v, sub ^ s, 0)
        return result

    def d_y(v):
        result = cy[0] * v
        for s in range(1, 4):
            result = result + cy[s] * along(v, lane ^ s, 1)
        return result

    def to_faces(v):
        ends = along(v, z_from, 0)
        return jnp.stack([jnp.where(lower, v[0], v[1]), jnp.where(z_first, ends[0], ends[1])])

    def to_nodes(f):
        z0 = along(f[1], z_index, 0)
        z1 = along(f[1], z_index + 2, 0)
        return jnp.stack([f[0] * x_node[0] + z0 * z_edge, f[0] * x_node[1] + z1 * z_edge])

    for copy in packs:
        copy.wait()
    pl.semaphore_wait(barrier, 4)
    sends1 = []
    for n, target in enumerate(targets):
        axis, from_up = n // 2, n % 2 == 0
        sends1.append(
            pltpu.make_async_remote_copy(
                src_ref=face.at[axis, :, up if from_up else low],
                dst_ref=recv1.at[axis, :, low if from_up else up],
                send_sem=s1.at[n],
                recv_sem=r1.at[n],
                device_id=target,
                device_id_type=MESH,
            )
        )
    for copy in sends1:
        copy.start()

    for copy in loads:
        copy.wait()
    lead, lane_one, row_two, lane_three = [], [], [], []
    for axis in range(2):
        word = codes[2 * axis + 1] + 8 * codes[2 * axis]
        word = jnp.where(
            lax.broadcasted_iota(jnp.int32, (8, 32), 0) < 4,
            jnp.broadcast_to(word[0:1], (8, 32)),
            jnp.broadcast_to(word[1:2], (8, 32)),
        )
        word = along(jnp.concatenate([word] * 4, 1), lane >> 2, 1)
        first, second = (word & 1) * 3, ((word >> 1) & 1) * 3
        swap = (word & 4) != 0
        lead.append((word & 8) != 0)
        lane_one.append(lane ^ jnp.where(swap, row ^ first ^ second, second))
        row_two.append(
            sub ^ jnp.where(swap, col ^ jnp.where(lower, first, second), first)
        )
        lane_three.append(lane ^ jnp.where(swap, row, 0))

    def orient(axis, layer):
        layer = along(layer, lane_one[axis], 1)
        layer = along(layer, row_two[axis], 0)
        return along(layer, lane_three[axis], 1)

    state = [nodes[k] for k in range(5)]
    metric = [[metv[g, d] for d in range(3)] for g in range(3)]
    velocity, pressure, warm = primitives(state)
    lifted = jnp.stack(velocity + [warm])
    inverse_j = 1.0 / jacv[...]

    def products(g):
        return (lifted[:, None] * jnp.stack(metric[g])[None]).reshape(12, 2, 8, 128)

    partial = d_x(products(0)) + d_z(products(1)) + d_y(products(2))
    y_normal = [along(metric[2][d], y_lead, 1) for d in range(3)]
    y_sums = [
        y_side * (lifted[k] + (wall_sign if k < 3 else 1.0) * along(lifted[k], y_other, 1))
        for k in range(4)
    ]
    partial = [
        [partial[3 * k + d] + y_sums[k] * y_normal[d] for d in range(3)] for k in range(4)
    ]
    scaled = visc_coef * inverse_j
    face_partial = [[to_faces(partial[k][d]) for d in range(3)] for k in range(4)]
    face_scaled = to_faces(scaled)
    own = [face[:, k] for k in range(8)]
    own_velocity, own_pressure, own_warm = primitives(own)
    own_lifted = own_velocity + [own_warm]

    for copy in sends1:
        copy.wait_recv()
    other = [
        jnp.stack([orient(axis, recv1[axis, k]) for axis in range(2)]) for k in range(8)
    ]
    leads = jnp.stack(lead)
    normal = [jnp.where(leads, own[5 + d], other[5 + d]) for d in range(3)]
    other_velocity, other_pressure, other_warm = primitives(other)
    other_lifted = other_velocity + [other_warm]
    sums = [(3.0 * side) * (own_lifted[k] + other_lifted[k]) for k in range(4)]

    def crossed(f):
        return jnp.stack([along(f[1], cross_index, 0), along(f[0], cross_index, 0)])

    cross_sums = [z_edge * crossed(sums[k]) for k in range(4)]
    cross_normal = [crossed(normal[d]) for d in range(3)]
    face_slopes = [
        [
            face_scaled
            * (face_partial[k][d] + sums[k] * normal[d] + cross_sums[k] * cross_normal[d])
            for d in range(3)
        ]
        for k in range(4)
    ]
    moment, energy = fluxes(own, own_velocity, own_pressure, face_slopes)
    own_half = [dot3(moment[j], normal) for j in range(3)] + [dot3(energy, normal)]
    for k in range(4):
        send2[:, k] = own_half[k]

    sends2 = []
    for n, target in enumerate(targets):
        axis, from_up = n // 2, n % 2 == 0
        sends2.append(
            pltpu.make_async_remote_copy(
                src_ref=send2.at[axis, :, up if from_up else low],
                dst_ref=recv2.at[axis, :, low if from_up else up],
                send_sem=s2.at[n],
                recv_sem=r2.at[n],
                device_id=target,
                device_id_type=MESH,
            )
        )
    for copy in sends2:
        copy.start()

    z_sums = [jnp.stack([along(sums[k][1], z_index, 0), along(sums[k][1], z_index + 2, 0)]) * z_edge for k in range(4)]
    z_normal = [jnp.stack([along(normal[d][1], z_index, 0), along(normal[d][1], z_index + 2, 0)]) for d in range(3)]
    x_mask = jnp.stack(x_node)
    slopes = [
        [
            scaled
            * (
                partial[k][d]
                + x_mask * (sums[k][0] * normal[d][0])
                + z_sums[k] * z_normal[d]
            )
            for d in range(3)
        ]
        for k in range(4)
    ]
    moment, energy = fluxes(state, velocity, pressure, slopes)

    def through(rows):
        parts = [dot3(state[1:4], rows)]
        parts += [dot3(moment[j], rows) for j in range(3)]
        return parts + [dot3(energy, rows)]

    total = d_x(jnp.stack(through(metric[0])))
    total = total + d_z(jnp.stack(through(metric[1])))
    total = total + d_y(jnp.stack(through(metric[2])))

    half_y = through(y_normal)
    heat_y = (-2.0 * heat_ratio) * dot3(slopes[3], y_normal)
    size_y = jnp.sqrt(dot3(y_normal, y_normal))
    speed = wave(velocity, jnp.sqrt(gamma_gas * warm), y_normal, size_y)
    speed = y_jump * jnp.maximum(speed, along(speed, y_other, 1))
    y_terms = []
    for k in range(5):
        sign = wall_sign if 1 <= k <= 3 else 1.0
        jump = sign * along(state[k], y_other, 1) - state[k]
        sign = wall_sign if k == 0 else 1.0
        both = half_y[k] + sign * along(half_y[k], y_other, 1)
        if k == 4:
            both = jnp.where(wall, heat_y, both)
        y_terms.append(y_side * both - speed * jump)

    size = jnp.sqrt(dot3(normal, normal))
    speed = jnp.maximum(
        wave(own_velocity, jnp.sqrt(gamma_gas * own_warm), normal, size),
        wave(other_velocity, jnp.sqrt(gamma_gas * other_warm), normal, size),
    )
    known = [dot3([own[1 + d] + other[1 + d] for d in range(3)], normal)] + own_half
    known = [
        (3.0 * side) * known[k] - (3.0 * speed) * (other[k] - own[k]) for k in range(5)
    ]
    out[0] = -inverse_j * (total[0] + y_terms[0] + to_nodes(known[0]))
    rest = [total[k] + y_terms[k] + to_nodes(known[k]) for k in range(1, 5)]

    for copy in sends2:
        copy.wait_recv()
    for k in range(4):
        arrived = jnp.stack([orient(axis, recv2[axis, k]) for axis in range(2)])
        out[1 + k] = -inverse_j * (rest[k] + to_nodes((3.0 * side) * arrived))
    for copy in sends1 + sends2:
        copy.wait_send()


def local(nx, nz, conserved, jacobian, metric, x_master, x_flip, z_master, z_flip):
    anywhere = pl.BlockSpec(memory_space=pl.ANY)
    words = [v.reshape(2, 32) for v in (x_master, x_flip, z_master, z_flip)]
    result = pl.pallas_call(
        functools.partial(kernel, nx, nz),
        out_shape=pltpu.VMEM((5, 2, 8, 128), jnp.float32),
        in_specs=[anywhere] * 9,
        out_specs=pl.BlockSpec(memory_space=pltpu.VMEM),
        scratch_shapes=[
            pltpu.VMEM((5, 2, 8, 128), jnp.float32),
            pltpu.VMEM((3, 3, 2, 8, 128), jnp.float32),
            pltpu.VMEM((2, 8, 128), jnp.float32),
            pltpu.VMEM((2, 8, 8, 128), jnp.float32),
            pltpu.VMEM((2, 8, 8, 128), jnp.float32),
            pltpu.VMEM((2, 4, 8, 128), jnp.float32),
            pltpu.VMEM((2, 4, 8, 128), jnp.float32),
            pltpu.VMEM((4, 2, 32), jnp.int32),
            pltpu.SemaphoreType.DMA((8,)),
            pltpu.SemaphoreType.DMA((7,)),
            pltpu.SemaphoreType.DMA((4,)),
            pltpu.SemaphoreType.DMA((4,)),
            pltpu.SemaphoreType.DMA((4,)),
            pltpu.SemaphoreType.DMA((4,)),
        ],
        compiler_params=pltpu.CompilerParams(collective_id=0, has_side_effects=True),
    )(
        conserved.reshape(5, 2, 8, 128),
        metric.reshape(3, 3, 2, 8, 128),
        jacobian.reshape(2, 8, 128),
        conserved,
        metric,
        *words,
    )
    return result.reshape(5, 4, 4, 128)


def solution(mesh):
    flags = P("gx", "gz", None)
    in_specs = (P(None, "gx", "gz", None), flags, P(None, None, "gx", "gz", None)) + (flags,) * 4
    return jax.shard_map(
        functools.partial(local, mesh.shape["gx"], mesh.shape["gz"]),
        mesh=mesh,
        in_specs=in_specs,
        out_specs=P(None, "gx", "gz", None),
        check_vma=False,
    )
```

```python
import functools
import math

import jax
import jax.numpy as jnp
import numpy as np
from jax import lax
from jax.experimental import pallas as pl
from jax.experimental.pallas import tpu as pltpu
from jax.sharding import PartitionSpec as P

MESH = pl.DeviceIdType.MESH
gamma_gas = 1.4
visc_coef = 0.1
prandtl = 0.72
heat_ratio = gamma_gas / ((gamma_gas - 1.0) * prandtl)


def node_table():
    points = np.array([-1.0, -math.sqrt(0.2), math.sqrt(0.2), 1.0])
    scales = np.array(
        [np.prod([points[r] - points[s] for s in range(4) if s != r]) for r in range(4)]
    )
    table = np.zeros((4, 4))
    for r in range(4):
        for c in range(4):
            if r != c:
                table[r, c] = scales[r] / (scales[c] * (points[r] - points[c]))
        table[r, r] = -np.sum(table[r])
    return table


weak = node_table()
weak[0, 0] += 6.0
weak[3, 3] -= 6.0


def pick(index, values):
    result = jnp.full(index.shape, float(values[3]), jnp.float32)
    for at in range(3):
        result = jnp.where(index == at, float(values[at]), result)
    return result


def along(values, index, axis):
    shape = values.shape
    flat = values.reshape((-1, 8, 128))
    parts = [
        jnp.take_along_axis(flat[n], index, axis=axis, mode="promise_in_bounds")
        for n in range(flat.shape[0])
    ]
    return jnp.stack(parts).reshape(shape)


def primitives(state):
    inverse = 1.0 / state[0]
    velocity = [state[1 + j] * inverse for j in range(3)]
    kinetic = state[1] * velocity[0] + state[2] * velocity[1] + state[3] * velocity[2]
    pressure = (gamma_gas - 1.0) * (state[4] - 0.5 * kinetic)
    return velocity, pressure, pressure * inverse


def dot3(left, right):
    return left[0] * right[0] + left[1] * right[1] + left[2] * right[2]


def fluxes(state, velocity, pressure, slopes):
    third = (2.0 / 3.0) * (slopes[0][0] + slopes[1][1] + slopes[2][2])
    stress = [[None] * 3 for _ in range(3)]
    moment = [[None] * 3 for _ in range(3)]
    for j in range(3):
        for d in range(j, 3):
            tau = slopes[j][d] + slopes[d][j]
            flow = state[1 + j] * velocity[d]
            if j == d:
                tau = tau - third
                flow = flow + pressure
            stress[j][d] = stress[d][j] = tau
            moment[j][d] = moment[d][j] = flow - tau
    total = state[4] + pressure
    energy = [
        total * velocity[d] - dot3(velocity, stress[d]) - heat_ratio * slopes[3][d]
        for d in range(3)
    ]
    return moment, energy


def wave(velocity, sound, normal, size):
    return jnp.abs(dot3(velocity, normal)) + sound * size


def kernel(
    nx, nz, cons_n, met_n, jac_n, cons_f, met_f, xm, xf, zm, zf, out,
    nodes, metv, jacv, face, recv, edge, corner, codes, lsem, csem, ssem, rsem,
):
    gx, gz = lax.axis_index("gx"), lax.axis_index("gz")
    x_to = [lax.rem(gx + nx - 1, nx), gx, lax.rem(gx + 1, nx)]
    z_to = [lax.rem(gz + nz - 1, nz), gz, lax.rem(gz + 1, nz)]
    sides = [(1, 0), (-1, 0), (0, 1), (0, -1)]
    diagonals = [(1, 1), (1, -1), (-1, 1), (-1, -1)]
    target = lambda way: (x_to[way[0] + 1], z_to[way[1] + 1])

    corner[...] = jnp.zeros_like(corner)
    barrier = pltpu.get_barrier_semaphore()
    for way in sides + diagonals:
        pl.semaphore_signal(barrier, inc=1, device_id=target(way), device_id_type=MESH)

    low, up = pl.ds(0, 4), pl.ds(4, 4)
    five, three = pl.ds(0, 5), pl.ds(5, 3)
    loads = [(cons_n, nodes), (met_n, metv), (jac_n, jacv)]
    loads += [(ref, codes.at[n]) for n, ref in enumerate((xm, xf, zm, zf))]
    loads = [pltpu.make_async_copy(a, b, csem.at[n]) for n, (a, b) in enumerate(loads)]
    packs = [
        (cons_f.at[:, 0], face.at[0, five, low]),
        (cons_f.at[:, 3], face.at[0, five, up]),
        (met_f.at[0, :, 0], face.at[0, three, low]),
        (met_f.at[0, :, 3], face.at[0, three, up]),
        (cons_f.at[:, :, 0, :], face.at[1, five, low]),
        (cons_f.at[:, :, 3, :], face.at[1, five, up]),
        (met_f.at[1, :, :, 0, :], face.at[1, three, low]),
        (met_f.at[1, :, :, 3, :], face.at[1, three, up]),
    ]
    packs = [pltpu.make_async_copy(a, b, lsem.at[n]) for n, (a, b) in enumerate(packs)]
    for copy in loads + packs:
        copy.start()

    sub = lax.broadcasted_iota(jnp.int32, (8, 128), 0)
    lane = lax.broadcasted_iota(jnp.int32, (8, 128), 1)
    row, col = sub & 3, lane & 3
    lower = sub < 4
    half = sub >> 2
    side = jnp.where(lower, -1.0, 1.0)
    x_node = [jnp.where(lower, 1.0, 0.0), jnp.where(lower, 0.0, 1.0)]
    z_edge = jnp.where((row == 0) | (row == 3), 1.0, 0.0)
    cross_index = half * 3 + jnp.where(row == 3, 4, 0)
    z_index = half + jnp.where(row == 3, 4, 0)
    z_from = ((sub & 1) << 2) + half * 3
    z_first = row < 2
    cz = [pick(row, [weak[a, a ^ s] for a in range(4)]) for s in range(4)]
    cy = [pick(col, [weak[a, a ^ s] for a in range(4)]) for s in range(4)]
    cx = [
        [
            [
                jnp.where(lower, float(weak[2 * v, 2 * w + s]), float(weak[2 * v + 1, 2 * w + 1 - s]))
                for s in range(2)
            ]
            for w in range(2)
        ]
        for v in range(2)
    ]
    wall = (lane == 0) | (lane == 127)
    wall_sign = jnp.where(wall, -1.0, 1.0)
    y_other = jnp.where(
        wall, lane, jnp.where(col == 0, lane - 1, jnp.where(col == 3, lane + 1, lane))
    )
    y_lead = jnp.where((col == 0) & (lane > 0), lane - 1, lane)
    y_side = jnp.where(col == 0, -3.0, jnp.where(col == 3, 3.0, 0.0))
    y_jump = jnp.abs(y_side)
    edge_side = jnp.where(row == 0, -3.0, jnp.where(row == 3, 3.0, 0.0))

    def d_x(v):
        r = jnp.stack([pltpu.roll(v[n], 4, 1) for n in range(v.shape[0])])
        parts = [
            cx[n][0][0] * v[:, 0] + cx[n][0][1] * r[:, 0] + cx[n][1][0] * v[:, 1] + cx[n][1][1] * r[:, 1]
            for n in range(2)
        ]
        return jnp.stack(parts, 1)

    def d_z(v):
        result = cz[0] * v
        for s in range(1, 4):
            result = result + cz[s] * along(v, sub ^ s, 0)
        return result

    def d_y(v):
        result = cy[0] * v
        for s in range(1, 4):
            result = result + cy[s] * along(v, lane ^ s, 1)
        return result

    def to_faces(v):
        ends = along(v, z_from, 0)
        return jnp.stack([jnp.where(lower, v[0], v[1]), jnp.where(z_first, ends[0], ends[1])])

    def to_nodes(f):
        z0 = along(f[1], z_index, 0)
        z1 = along(f[1], z_index + 2, 0)
        return jnp.stack([f[0] * x_node[0] + z0 * z_edge, f[0] * x_node[1] + z1 * z_edge])

    def crossed(f):
        return along(f, cross_index, 0)

    for copy in loads:
        copy.wait()
    lead, lead_edge, lane_one, row_in, row_out, lane_three = [], [], [], [], [], []
    rows_at = lax.broadcasted_iota(jnp.int32, (8, 32), 0)
    for axis in range(2):
        word = codes[2 * axis + 1] + 8 * codes[2 * axis]
        first = jnp.broadcast_to(word[0:1], (8, 32))
        second = jnp.broadcast_to(word[1:2], (8, 32))
        cross = jnp.where((rows_at & 3) < 2, first, second)
        word = jnp.where(rows_at < 4, first, second)
        cross = along(jnp.concatenate([cross] * 4, 1), lane >> 2, 1)
        word = along(jnp.concatenate([word] * 4, 1), lane >> 2, 1)
        first, second = (word & 1) * 3, ((word >> 1) & 1) * 3
        swap = (word & 4) != 0
        lead.append(word >> 3)
        lead_edge.append(cross >> 3)
        lane_one.append(lane ^ jnp.where(swap, row ^ first ^ second, second))
        row_in.append(sub ^ jnp.where(swap, col ^ jnp.where(lower, first, second), first))
        row_out.append(sub ^ jnp.where(swap, col ^ jnp.where(lower, second, first), first))
        lane_three.append(lane ^ jnp.where(swap, row, 0))
    lead = jnp.stack(lead).astype(jnp.float32)
    leads = lead > 0.5
    lead_edge = jnp.stack(lead_edge[::-1]).astype(jnp.float32)

    def orient(layers, row_two):
        parts = []
        for axis in range(2):
            layer = along(layers[axis], lane_one[axis], 1)
            layer = along(layer, row_two[axis], 0)
            parts.append(along(layer, lane_three[axis], 1))
        return jnp.stack(parts)

    state = [nodes[k] for k in range(5)]
    metric = [[metv[g, d] for d in range(3)] for g in range(3)]
    velocity, pressure, warm = primitives(state)
    lifted = jnp.stack(velocity + [warm])
    inverse_j = 1.0 / jacv[...]

    def products(g):
        return (lifted[:, None] * jnp.stack(metric[g])[None]).reshape(12, 2, 8, 128)

    partial = d_x(products(0)) + d_z(products(1)) + d_y(products(2))
    y_normal = [along(metric[2][d], y_lead, 1) for d in range(3)]
    y_sums = [
        y_side * (lifted[k] + (wall_sign if k < 3 else 1.0) * along(lifted[k], y_other, 1))
        for k in range(4)
    ]
    scaled = visc_coef * inverse_j
    partial = [
        [scaled * (partial[3 * k + d] + y_sums[k] * y_normal[d]) for d in range(3)]
        for k in range(4)
    ]
    face_partial = [[to_faces(partial[k][d]) for d in range(3)] for k in range(4)]
    face_scaled = to_faces(scaled)
    for k in range(4):
        for d in range(3):
            face[:, 8 + 3 * k + d] = face_partial[k][d]
    face[:, 20] = face_scaled
    for d in range(3):
        across = to_faces(metric[1][d])[0], to_faces(metric[0][d])[1]
        face[:, 21 + d] = lead_edge * jnp.stack(across)

    for copy in packs:
        copy.wait()
    own = [face[:, k] for k in range(8)]
    own_velocity, own_pressure, own_warm = primitives(own)
    own_lifted = own_velocity + [own_warm]
    seen = [orient(v, row_out) for v in own_lifted + [lead * own[5 + d] for d in range(3)]]
    for k in range(7):
        edge[0, k] = crossed(seen[k][0])
        edge[1, k] = seen[k][1]

    pl.semaphore_wait(barrier, 8)
    sends = []
    for n, way in enumerate(sides):
        axis, from_up = n // 2, n % 2 == 0
        sends.append(
            pltpu.make_async_remote_copy(
                src_ref=face.at[axis, :, up if from_up else low],
                dst_ref=recv.at[axis, :, low if from_up else up],
                send_sem=ssem.at[n],
                recv_sem=rsem.at[n],
                device_id=target(way),
                device_id_type=MESH,
            )
        )
    for n, way in enumerate(diagonals):
        at = (3 if way[0] > 0 else 0) + (4 if way[1] > 0 else 0)
        sends.append(
            pltpu.make_async_remote_copy(
                src_ref=edge.at[:, :, pl.ds(at, 1)],
                dst_ref=corner.at[:, :, pl.ds(7 - at, 1)],
                send_sem=ssem.at[4 + n],
                recv_sem=rsem.at[4 + n],
                device_id=target(way),
                device_id_type=MESH,
            )
        )
    for copy in sends[4:] + sends[:4]:
        copy.start()
    for copy in sends:
        copy.wait_recv()

    they = [recv[:, k] for k in range(8)]
    they_scaled = recv[:, 20]
    they_velocity, they_pressure, they_warm = primitives(they)
    they_lifted = they_velocity + [they_warm]
    they_normal = [jnp.where(leads, seen[4 + d], they[5 + d]) for d in range(3)]
    they_sums = [(-3.0 * side) * (they_lifted[k] + seen[k]) for k in range(4)]
    line = [jnp.stack([crossed(corner[1, k]), corner[0, k]]) for k in range(7)]
    line_sums = [edge_side * (they_lifted[k] + line[k]) for k in range(4)]
    line_normal = [recv[:, 21 + d] + line[4 + d] for d in range(3)]
    they_slopes = [
        [
            recv[:, 8 + 3 * k + d]
            + they_scaled * (they_sums[k] * they_normal[d] + line_sums[k] * line_normal[d])
            for d in range(3)
        ]
        for k in range(4)
    ]
    moment, energy = fluxes(they, they_velocity, they_pressure, they_slopes)
    they_half = [dot3(they[1:4], they_normal)]
    they_half += [dot3(moment[j], they_normal) for j in range(3)]
    they_half += [dot3(energy, they_normal)]
    they_size = jnp.sqrt(dot3(they_normal, they_normal))
    they_speed = wave(they_velocity, jnp.sqrt(gamma_gas * they_warm), they_normal, they_size)

    other = [orient(they[k], row_in) for k in range(5)]
    other_half = [orient(they_half[k], row_in) for k in range(5)]
    other_speed = orient(they_speed, row_in)
    sums = [-orient(they_sums[k], row_in) for k in range(4)]
    normal = [jnp.where(leads, own[5 + d], orient(they[5 + d], row_in)) for d in range(3)]

    def both_crossed(f):
        return jnp.stack([crossed(f[1]), crossed(f[0])])

    cross_sums = [z_edge * both_crossed(sums[k]) for k in range(4)]
    cross_normal = [both_crossed(normal[d]) for d in range(3)]
    face_slopes = [
        [
            face_partial[k][d]
            + face_scaled * (sums[k] * normal[d] + cross_sums[k] * cross_normal[d])
            for d in range(3)
        ]
        for k in range(4)
    ]
    moment, energy = fluxes(own, own_velocity, own_pressure, face_slopes)
    own_half = [dot3(own[1:4], normal)]
    own_half += [dot3(moment[j], normal) for j in range(3)] + [dot3(energy, normal)]
    own_speed = wave(
        own_velocity, jnp.sqrt(gamma_gas * own_warm), normal, jnp.sqrt(dot3(normal, normal))
    )
    speed = 3.0 * jnp.maximum(own_speed, other_speed)
    tile_terms = [
        (3.0 * side) * (own_half[k] + other_half[k]) - speed * (other[k] - own[k])
        for k in range(5)
    ]

    z_sums = [jnp.stack([along(sums[k][1], z_index, 0), along(sums[k][1], z_index + 2, 0)]) * z_edge for k in range(4)]
    z_normal = [jnp.stack([along(normal[d][1], z_index, 0), along(normal[d][1], z_index + 2, 0)]) for d in range(3)]
    x_mask = jnp.stack(x_node)
    slopes = [
        [
            partial[k][d]
            + scaled * (x_mask * (sums[k][0] * normal[d][0]) + z_sums[k] * z_normal[d])
            for d in range(3)
        ]
        for k in range(4)
    ]
    moment, energy = fluxes(state, velocity, pressure, slopes)

    def through(rows):
        parts = [dot3(state[1:4], rows)]
        parts += [dot3(moment[j], rows) for j in range(3)]
        return parts + [dot3(energy, rows)]

    total = d_x(jnp.stack(through(metric[0])))
    total = total + d_z(jnp.stack(through(metric[1])))
    total = total + d_y(jnp.stack(through(metric[2])))

    half_y = through(y_normal)
    heat_y = (-2.0 * heat_ratio) * dot3(slopes[3], y_normal)
    size_y = jnp.sqrt(dot3(y_normal, y_normal))
    speed = wave(velocity, jnp.sqrt(gamma_gas * warm), y_normal, size_y)
    speed = y_jump * jnp.maximum(speed, along(speed, y_other, 1))
    y_terms = []
    for k in range(5):
        sign = wall_sign if 1 <= k <= 3 else 1.0
        jump = sign * along(state[k], y_other, 1) - state[k]
        sign = wall_sign if k == 0 else 1.0
        both = half_y[k] + sign * along(half_y[k], y_other, 1)
        if k == 4:
            both = jnp.where(wall, heat_y, both)
        y_terms.append(y_side * both - speed * jump)

    for k in range(5):
        out[k] = -inverse_j * (total[k] + y_terms[k] + to_nodes(tile_terms[k]))
    for copy in sends:
        copy.wait_send()


def local(nx, nz, conserved, jacobian, metric, x_master, x_flip, z_master, z_flip):
    anywhere = pl.BlockSpec(memory_space=pl.ANY)
    words = [v.reshape(2, 32) for v in (x_master, x_flip, z_master, z_flip)]
    result = pl.pallas_call(
        functools.partial(kernel, nx, nz),
        out_shape=pltpu.VMEM((5, 2, 8, 128), jnp.float32),
        in_specs=[anywhere] * 9,
        out_specs=pl.BlockSpec(memory_space=pltpu.VMEM),
        scratch_shapes=[
            pltpu.VMEM((5, 2, 8, 128), jnp.float32),
            pltpu.VMEM((3, 3, 2, 8, 128), jnp.float32),
            pltpu.VMEM((2, 8, 128), jnp.float32),
            pltpu.VMEM((2, 24, 8, 128), jnp.float32),
            pltpu.VMEM((2, 24, 8, 128), jnp.float32),
            pltpu.VMEM((2, 7, 8, 128), jnp.float32),
            pltpu.VMEM((2, 7, 8, 128), jnp.float32),
            pltpu.VMEM((4, 2, 32), jnp.int32),
            pltpu.SemaphoreType.DMA((8,)),
            pltpu.SemaphoreType.DMA((7,)),
            pltpu.SemaphoreType.DMA((8,)),
            pltpu.SemaphoreType.DMA((8,)),
        ],
        compiler_params=pltpu.CompilerParams(collective_id=0, has_side_effects=True),
    )(
        conserved.reshape(5, 2, 8, 128),
        metric.reshape(3, 3, 2, 8, 128),
        jacobian.reshape(2, 8, 128),
        conserved,
        metric,
        *words,
    )
    return result.reshape(5, 4, 4, 128)


def solution(mesh):
    flags = P("gx", "gz", None)
    in_specs = (P(None, "gx", "gz", None), flags, P(None, None, "gx", "gz", None)) + (flags,) * 4
    return jax.shard_map(
        functools.partial(local, mesh.shape["gx"], mesh.shape["gz"]),
        mesh=mesh,
        in_specs=in_specs,
        out_specs=P(None, "gx", "gz", None),
        check_vma=False,
    )
```

```python
import functools
import math

import jax
import jax.numpy as jnp
import numpy as np
from jax import lax
from jax.experimental import pallas as pl
from jax.experimental.pallas import tpu as pltpu
from jax.sharding import PartitionSpec as P

MESH = pl.DeviceIdType.MESH
gamma_gas = 1.4
visc_coef = 0.1
prandtl = 0.72
heat_ratio = gamma_gas / ((gamma_gas - 1.0) * prandtl)


def node_table():
    points = np.array([-1.0, -math.sqrt(0.2), math.sqrt(0.2), 1.0])
    scales = np.array(
        [np.prod([points[r] - points[s] for s in range(4) if s != r]) for r in range(4)]
    )
    table = np.zeros((4, 4))
    for r in range(4):
        for c in range(4):
            if r != c:
                table[r, c] = scales[r] / (scales[c] * (points[r] - points[c]))
        table[r, r] = -np.sum(table[r])
    return table


weak = node_table()
weak[0, 0] += 6.0
weak[3, 3] -= 6.0


def pick(index, values):
    result = jnp.full(index.shape, float(values[3]), jnp.float32)
    for at in range(3):
        result = jnp.where(index == at, float(values[at]), result)
    return result


def along(values, index, axis):
    shape = values.shape
    flat = values.reshape((-1, 8, 128))
    parts = [
        jnp.take_along_axis(flat[n], index, axis=axis, mode="promise_in_bounds")
        for n in range(flat.shape[0])
    ]
    return jnp.stack(parts).reshape(shape)


def primitives(state):
    inverse = 1.0 / state[0]
    velocity = [state[1 + j] * inverse for j in range(3)]
    kinetic = state[1] * velocity[0] + state[2] * velocity[1] + state[3] * velocity[2]
    pressure = (gamma_gas - 1.0) * (state[4] - 0.5 * kinetic)
    return velocity, pressure, pressure * inverse


def dot3(left, right):
    return left[0] * right[0] + left[1] * right[1] + left[2] * right[2]


def flows(state, velocity, pressure):
    moment = [[None] * 3 for _ in range(3)]
    for j in range(3):
        for d in range(j, 3):
            flow = state[1 + j] * velocity[d]
            moment[j][d] = moment[d][j] = flow + pressure if j == d else flow
    total = state[4] + pressure
    return moment, [total * velocity[d] for d in range(3)]


def fluxes(inviscid, velocity, slopes):
    third = (2.0 / 3.0) * (slopes[0][0] + slopes[1][1] + slopes[2][2])
    stress = [[None] * 3 for _ in range(3)]
    moment = [[None] * 3 for _ in range(3)]
    for j in range(3):
        for d in range(j, 3):
            tau = slopes[j][d] + slopes[d][j]
            if j == d:
                tau = tau - third
            stress[j][d] = stress[d][j] = tau
            moment[j][d] = moment[d][j] = inviscid[0][j][d] - tau
    energy = [
        inviscid[1][d] - dot3(velocity, stress[d]) - heat_ratio * slopes[3][d]
        for d in range(3)
    ]
    return moment, energy


def wave(velocity, sound, normal, size):
    return jnp.abs(dot3(velocity, normal)) + sound * size


def kernel(
    nx, nz, cons_n, met_n, jac_n, xm, xf, zm, zf, out,
    nodes, metv, jacv, face, recv, edge, corner, codes, csem, ssem, rsem,
):
    gx, gz = lax.axis_index("gx"), lax.axis_index("gz")
    x_to = [lax.rem(gx + nx - 1, nx), gx, lax.rem(gx + 1, nx)]
    z_to = [lax.rem(gz + nz - 1, nz), gz, lax.rem(gz + 1, nz)]
    sides = [(1, 0), (-1, 0), (0, 1), (0, -1)]
    diagonals = [(1, 1), (1, -1), (-1, 1), (-1, -1)]
    target = lambda way: (x_to[way[0] + 1], z_to[way[1] + 1])

    corner[...] = jnp.zeros_like(corner)
    barrier = pltpu.get_barrier_semaphore()
    for way in diagonals + sides[::-1]:
        pl.semaphore_signal(barrier, inc=1, device_id=target(way), device_id_type=MESH)

    low, up = pl.ds(0, 4), pl.ds(4, 4)
    loads = [(ref, codes.at[n]) for n, ref in enumerate((xm, xf, zm, zf))]
    loads += [(cons_n, nodes), (met_n, metv), (jac_n, jacv)]
    loads = [pltpu.make_async_copy(a, b, csem.at[n]) for n, (a, b) in enumerate(loads)]
    for copy in loads:
        copy.start()

    sub = lax.broadcasted_iota(jnp.int32, (8, 128), 0)
    lane = lax.broadcasted_iota(jnp.int32, (8, 128), 1)
    row, col = sub & 3, lane & 3
    lower = sub < 4
    half = sub >> 2
    side = jnp.where(lower, -1.0, 1.0)
    x_node = [jnp.where(lower, 1.0, 0.0), jnp.where(lower, 0.0, 1.0)]
    z_edge = jnp.where((row == 0) | (row == 3), 1.0, 0.0)
    cross_index = half * 3 + jnp.where(row == 3, 4, 0)
    z_index = half + jnp.where(row == 3, 4, 0)
    z_from = ((sub & 1) << 2) + half * 3
    z_first = row < 2
    cz = [pick(row, [weak[a, a ^ s] for a in range(4)]) for s in range(4)]
    cy = [pick(col, [weak[a, a ^ s] for a in range(4)]) for s in range(4)]
    cx = [
        [
            [
                jnp.where(lower, float(weak[2 * v, 2 * w + s]), float(weak[2 * v + 1, 2 * w + 1 - s]))
                for s in range(2)
            ]
            for w in range(2)
        ]
        for v in range(2)
    ]
    wall = (lane == 0) | (lane == 127)
    wall_sign = jnp.where(wall, -1.0, 1.0)
    y_other = jnp.where(
        wall, lane, jnp.where(col == 0, lane - 1, jnp.where(col == 3, lane + 1, lane))
    )
    y_lead = jnp.where((col == 0) & (lane > 0), lane - 1, lane)
    y_side = jnp.where(col == 0, -3.0, jnp.where(col == 3, 3.0, 0.0))
    y_jump = jnp.abs(y_side)
    edge_side = jnp.where(row == 0, -3.0, jnp.where(row == 3, 3.0, 0.0))

    def d_x(v):
        r = jnp.stack([pltpu.roll(v[n], 4, 1) for n in range(v.shape[0])])
        parts = [
            cx[n][0][0] * v[:, 0] + cx[n][0][1] * r[:, 0] + cx[n][1][0] * v[:, 1] + cx[n][1][1] * r[:, 1]
            for n in range(2)
        ]
        return jnp.stack(parts, 1)

    def d_z(v):
        result = cz[0] * v
        for s in range(1, 4):
            result = result + cz[s] * along(v, sub ^ s, 0)
        return result

    def d_y(v):
        result = cy[0] * v
        for s in range(1, 4):
            result = result + cy[s] * along(v, lane ^ s, 1)
        return result

    def to_faces(v):
        ends = along(v, z_from, 0)
        return jnp.stack([jnp.where(lower, v[0], v[1]), jnp.where(z_first, ends[0], ends[1])])

    def to_nodes(f):
        z0 = along(f[1], z_index, 0)
        z1 = along(f[1], z_index + 2, 0)
        return jnp.stack([f[0] * x_node[0] + z0 * z_edge, f[0] * x_node[1] + z1 * z_edge])

    def crossed(f):
        return along(f, cross_index, 0)

    for copy in loads[:4]:
        copy.wait()
    lead, lead_edge, lane_one, row_in, row_out, lane_three = [], [], [], [], [], []
    rows_at = lax.broadcasted_iota(jnp.int32, (8, 32), 0)
    for axis in range(2):
        word = codes[2 * axis + 1] + 8 * codes[2 * axis]
        first = jnp.broadcast_to(word[0:1], (8, 32))
        second = jnp.broadcast_to(word[1:2], (8, 32))
        cross = jnp.where((rows_at & 3) < 2, first, second)
        word = jnp.where(rows_at < 4, first, second)
        cross = along(jnp.concatenate([cross] * 4, 1), lane >> 2, 1)
        word = along(jnp.concatenate([word] * 4, 1), lane >> 2, 1)
        first, second = (word & 1) * 3, ((word >> 1) & 1) * 3
        swap = (word & 4) != 0
        lead.append(word >> 3)
        lead_edge.append(cross >> 3)
        lane_one.append(lane ^ jnp.where(swap, row ^ first ^ second, second))
        row_in.append(sub ^ jnp.where(swap, col ^ jnp.where(lower, first, second), first))
        row_out.append(sub ^ jnp.where(swap, col ^ jnp.where(lower, second, first), first))
        lane_three.append(lane ^ jnp.where(swap, row, 0))
    lead = jnp.stack(lead).astype(jnp.float32)
    leads = lead > 0.5
    lead_edge = jnp.stack(lead_edge[::-1]).astype(jnp.float32)

    def orient(layers, row_two):
        parts = []
        for axis in range(2):
            layer = along(layers[axis], lane_one[axis], 1)
            layer = along(layer, row_two[axis], 0)
            parts.append(along(layer, lane_three[axis], 1))
        return jnp.stack(parts)

    loads[4].wait()
    state = [nodes[k] for k in range(5)]
    velocity, pressure, warm = primitives(state)
    lifted = jnp.stack(velocity + [warm])
    own_velocity = [to_faces(v) for v in velocity]
    own_warm = to_faces(warm)
    own_lifted = own_velocity + [own_warm]
    loads[5].wait()
    metric = [[metv[g, d] for d in range(3)] for g in range(3)]
    own_row = [
        jnp.stack([to_faces(metric[0][d])[0], to_faces(metric[1][d])[1]]) for d in range(3)
    ]
    seen = [orient(v, row_out) for v in own_lifted + [lead * own_row[d] for d in range(3)]]
    for k in range(7):
        edge[0, k] = crossed(seen[k][0])
        edge[1, k] = seen[k][1]

    pl.semaphore_wait(barrier, 8)
    corner_sends = []
    for n, way in enumerate(diagonals):
        at = (3 if way[0] > 0 else 0) + (4 if way[1] > 0 else 0)
        corner_sends.append(
            pltpu.make_async_remote_copy(
                src_ref=edge.at[:, :, pl.ds(at, 1)],
                dst_ref=corner.at[:, :, pl.ds(7 - at, 1)],
                send_sem=ssem.at[4 + n],
                recv_sem=rsem.at[4 + n],
                device_id=target(way),
                device_id_type=MESH,
            )
        )
    for copy in corner_sends:
        copy.start()

    def products(g):
        return (lifted[:, None] * jnp.stack(metric[g])[None]).reshape(12, 2, 8, 128)

    partial = d_x(products(0)) + d_z(products(1)) + d_y(products(2))
    y_normal = [along(metric[2][d], y_lead, 1) for d in range(3)]
    y_sums = [
        y_side * (lifted[k] + (wall_sign if k < 3 else 1.0) * along(lifted[k], y_other, 1))
        for k in range(4)
    ]
    loads[6].wait()
    inverse_j = 1.0 / jacv[...]
    scaled = visc_coef * inverse_j
    partial = [
        [scaled * (partial[3 * k + d] + y_sums[k] * y_normal[d]) for d in range(3)]
        for k in range(4)
    ]
    face_partial = [[to_faces(partial[k][d]) for d in range(3)] for k in range(4)]
    face_scaled = to_faces(scaled)
    own = [to_faces(state[k]) for k in range(5)]
    for k in range(5):
        face[:, k] = own[k]
    for d in range(3):
        face[:, 5 + d] = own_row[d]
    for k in range(4):
        for d in range(3):
            face[:, 8 + 3 * k + d] = face_partial[k][d]
    face[:, 20] = face_scaled
    for d in range(3):
        across = to_faces(metric[1][d])[0], to_faces(metric[0][d])[1]
        face[:, 21 + d] = lead_edge * jnp.stack(across)

    sends = []
    for n, way in enumerate(sides):
        axis, from_up = n // 2, n % 2 == 0
        sends.append(
            pltpu.make_async_remote_copy(
                src_ref=face.at[axis, :, up if from_up else low],
                dst_ref=recv.at[axis, :, low if from_up else up],
                send_sem=ssem.at[n],
                recv_sem=rsem.at[n],
                device_id=target(way),
                device_id_type=MESH,
            )
        )
    for copy in sends[::-1]:
        copy.start()

    inviscid = flows(state, velocity, pressure)
    own_inviscid = flows(own, own_velocity, to_faces(pressure))
    own_sound = jnp.sqrt(gamma_gas * own_warm)
    size_y = jnp.sqrt(dot3(y_normal, y_normal))
    speed = wave(velocity, jnp.sqrt(gamma_gas * warm), y_normal, size_y)
    speed = y_jump * jnp.maximum(speed, along(speed, y_other, 1))
    y_terms = []
    for k in range(5):
        sign = wall_sign if 1 <= k <= 3 else 1.0
        y_terms.append(speed * (state[k] - sign * along(state[k], y_other, 1)))
    mass_y = dot3(state[1:4], y_normal)
    mass_terms = y_terms[0] + y_side * (mass_y + wall_sign * along(mass_y, y_other, 1))
    mass_flux = [dot3(state[1:4], metric[g])[None] for g in range(3)]
    mass_terms = mass_terms + (d_x(mass_flux[0]) + d_z(mass_flux[1]) + d_y(mass_flux[2]))[0]
    mass_terms = -inverse_j * mass_terms

    for copy in sends:
        copy.wait_recv()

    they = [recv[:, k] for k in range(8)]
    they_scaled = recv[:, 20]
    they_velocity, they_pressure, they_warm = primitives(they)
    they_lifted = they_velocity + [they_warm]
    they_normal = [jnp.where(leads, seen[4 + d], they[5 + d]) for d in range(3)]
    they_sums = [(-3.0 * side) * (they_lifted[k] + seen[k]) for k in range(4)]
    they_slopes = [
        [
            recv[:, 8 + 3 * k + d]
            + (they_scaled * they_sums[k]) * they_normal[d]
            for d in range(3)
        ]
        for k in range(4)
    ]
    they_inviscid = flows(they, they_velocity, they_pressure)
    moment, energy = fluxes(they_inviscid, they_velocity, they_slopes)
    they_half = [dot3(they[1:4], they_normal)]
    they_half += [dot3(moment[j], they_normal) for j in range(3)]
    they_half += [dot3(energy, they_normal)]
    they_size = jnp.sqrt(dot3(they_normal, they_normal))
    they_speed = wave(they_velocity, jnp.sqrt(gamma_gas * they_warm), they_normal, they_size)

    other = [orient(they[k], row_in) for k in range(5)]
    other_half = [orient(they_half[k], row_in) for k in range(5)]
    other_speed = orient(they_speed, row_in)
    sums = [-orient(they_sums[k], row_in) for k in range(4)]
    normal = [jnp.where(leads, own_row[d], orient(they[5 + d], row_in)) for d in range(3)]

    def both_crossed(f):
        return jnp.stack([crossed(f[1]), crossed(f[0])])

    cross_sums = [z_edge * both_crossed(sums[k]) for k in range(4)]
    cross_normal = [both_crossed(normal[d]) for d in range(3)]
    face_slopes = [
        [
            face_partial[k][d]
            + face_scaled * (sums[k] * normal[d] + cross_sums[k] * cross_normal[d])
            for d in range(3)
        ]
        for k in range(4)
    ]
    moment, energy = fluxes(own_inviscid, own_velocity, face_slopes)
    own_half = [dot3(own[1:4], normal)]
    own_half += [dot3(moment[j], normal) for j in range(3)] + [dot3(energy, normal)]
    own_speed = wave(own_velocity, own_sound, normal, jnp.sqrt(dot3(normal, normal)))
    speed = 3.0 * jnp.maximum(own_speed, other_speed)
    tile_terms = [
        (3.0 * side) * (own_half[k] + other_half[k]) - speed * (other[k] - own[k])
        for k in range(5)
    ]

    z_sums = [jnp.stack([along(sums[k][1], z_index, 0), along(sums[k][1], z_index + 2, 0)]) * z_edge for k in range(4)]
    z_normal = [jnp.stack([along(normal[d][1], z_index, 0), along(normal[d][1], z_index + 2, 0)]) for d in range(3)]
    x_mask = jnp.stack(x_node)
    slopes = [
        [
            partial[k][d]
            + scaled * (x_mask * (sums[k][0] * normal[d][0]) + z_sums[k] * z_normal[d])
            for d in range(3)
        ]
        for k in range(4)
    ]
    moment, energy = fluxes(inviscid, velocity, slopes)

    def through(rows):
        return [dot3(moment[j], rows) for j in range(3)] + [dot3(energy, rows)]

    total = d_x(jnp.stack(through(metric[0])))
    total = total + d_z(jnp.stack(through(metric[1])))
    total = total + d_y(jnp.stack(through(metric[2])))

    half_y = through(y_normal)
    heat_y = (-2.0 * heat_ratio) * dot3(slopes[3], y_normal)
    for k in range(4):
        both = half_y[k] + along(half_y[k], y_other, 1)
        if k == 3:
            both = jnp.where(wall, heat_y, both)
        y_terms[1 + k] = y_terms[1 + k] + y_side * both
    out[0] = mass_terms - inverse_j * to_nodes(tile_terms[0])
    ready = [
        -inverse_j * (total[k] + y_terms[1 + k] + to_nodes(tile_terms[1 + k])) for k in range(4)
    ]

    for copy in corner_sends:
        copy.wait_recv()
    line = [jnp.stack([crossed(corner[1, k]), corner[0, k]]) for k in range(7)]
    line_sums = [
        (edge_side * they_scaled) * (they_lifted[k] + line[k]) for k in range(4)
    ]
    line_normal = [recv[:, 21 + d] + line[4 + d] for d in range(3)]
    onto = dot3(line_normal, they_normal)
    carried = dot3(line_sums, they_normal)
    spread = (2.0 / 3.0) * dot3(line_sums, line_normal)
    drag = [
        spread * they_normal[j] - line_sums[j] * onto - line_normal[j] * carried
        for j in range(3)
    ]
    drag.append(dot3(they_velocity, drag) - heat_ratio * (line_sums[3] * onto))
    for k in range(4):
        late = (3.0 * side) * orient(drag[k], row_in)
        out[1 + k] = ready[k] - inverse_j * to_nodes(late)
    for copy in sends + corner_sends:
        copy.wait_send()


def local(nx, nz, conserved, jacobian, metric, x_master, x_flip, z_master, z_flip):
    anywhere = pl.BlockSpec(memory_space=pl.ANY)
    words = [v.reshape(2, 32) for v in (x_master, x_flip, z_master, z_flip)]
    result = pl.pallas_call(
        functools.partial(kernel, nx, nz),
        out_shape=pltpu.VMEM((5, 2, 8, 128), jnp.float32),
        in_specs=[anywhere] * 7,
        out_specs=pl.BlockSpec(memory_space=pltpu.VMEM),
        scratch_shapes=[
            pltpu.VMEM((5, 2, 8, 128), jnp.float32),
            pltpu.VMEM((3, 3, 2, 8, 128), jnp.float32),
            pltpu.VMEM((2, 8, 128), jnp.float32),
            pltpu.VMEM((2, 24, 8, 128), jnp.float32),
            pltpu.VMEM((2, 24, 8, 128), jnp.float32),
            pltpu.VMEM((2, 7, 8, 128), jnp.float32),
            pltpu.VMEM((2, 7, 8, 128), jnp.float32),
            pltpu.VMEM((4, 2, 32), jnp.int32),
            pltpu.SemaphoreType.DMA((7,)),
            pltpu.SemaphoreType.DMA((8,)),
            pltpu.SemaphoreType.DMA((8,)),
        ],
        compiler_params=pltpu.CompilerParams(collective_id=0, has_side_effects=True),
    )(
        conserved.reshape(5, 2, 8, 128),
        metric.reshape(3, 3, 2, 8, 128),
        jacobian.reshape(2, 8, 128),
        *words,
    )
    return result.reshape(5, 4, 4, 128)


def solution(mesh):
    flags = P("gx", "gz", None)
    in_specs = (P(None, "gx", "gz", None), flags, P(None, None, "gx", "gz", None)) + (flags,) * 4
    return jax.shard_map(
        functools.partial(local, mesh.shape["gx"], mesh.shape["gz"]),
        mesh=mesh,
        in_specs=in_specs,
        out_specs=P(None, "gx", "gz", None),
        check_vma=False,
    )
```

```python
import functools
import math

import jax
import jax.numpy as jnp
import numpy as np
from jax import lax
from jax.experimental import pallas as pl
from jax.experimental.pallas import tpu as pltpu
from jax.sharding import PartitionSpec as P

MESH = pl.DeviceIdType.MESH
gamma_gas = 1.4
visc_coef = 0.1
prandtl = 0.72
heat_ratio = gamma_gas / ((gamma_gas - 1.0) * prandtl)


def node_table():
    points = np.array([-1.0, -math.sqrt(0.2), math.sqrt(0.2), 1.0])
    scales = np.array(
        [np.prod([points[r] - points[s] for s in range(4) if s != r]) for r in range(4)]
    )
    table = np.zeros((4, 4))
    for r in range(4):
        for c in range(4):
            if r != c:
                table[r, c] = scales[r] / (scales[c] * (points[r] - points[c]))
        table[r, r] = -np.sum(table[r])
    return table


weak = node_table()
weak[0, 0] += 6.0
weak[3, 3] -= 6.0


def pick(index, values):
    result = jnp.full(index.shape, float(values[3]), jnp.float32)
    for at in range(3):
        result = jnp.where(index == at, float(values[at]), result)
    return result


def along(values, index, axis):
    shape = values.shape
    flat = values.reshape((-1, 8, 128))
    parts = [
        jnp.take_along_axis(flat[n], index, axis=axis, mode="promise_in_bounds")
        for n in range(flat.shape[0])
    ]
    return jnp.stack(parts).reshape(shape)


def primitives(state):
    inverse = 1.0 / state[0]
    velocity = [state[1 + j] * inverse for j in range(3)]
    kinetic = state[1] * velocity[0] + state[2] * velocity[1] + state[3] * velocity[2]
    pressure = (gamma_gas - 1.0) * (state[4] - 0.5 * kinetic)
    return velocity, pressure, pressure * inverse


def dot3(left, right):
    return left[0] * right[0] + left[1] * right[1] + left[2] * right[2]


def flows(state, velocity, pressure):
    moment = [[None] * 3 for _ in range(3)]
    for j in range(3):
        for d in range(j, 3):
            flow = state[1 + j] * velocity[d]
            moment[j][d] = moment[d][j] = flow + pressure if j == d else flow
    total = state[4] + pressure
    return moment, [total * velocity[d] for d in range(3)]


def fluxes(inviscid, velocity, slopes):
    third = (2.0 / 3.0) * (slopes[0][0] + slopes[1][1] + slopes[2][2])
    stress = [[None] * 3 for _ in range(3)]
    moment = [[None] * 3 for _ in range(3)]
    for j in range(3):
        for d in range(j, 3):
            tau = slopes[j][d] + slopes[d][j]
            if j == d:
                tau = tau - third
            stress[j][d] = stress[d][j] = tau
            moment[j][d] = moment[d][j] = inviscid[0][j][d] - tau
    energy = [
        inviscid[1][d] - dot3(velocity, stress[d]) - heat_ratio * slopes[3][d]
        for d in range(3)
    ]
    return moment, energy


def wave(velocity, sound, normal, size):
    return jnp.abs(dot3(velocity, normal)) + sound * size


def kernel(
    nx, nz, cons_n, met_n, jac_n, xm, xf, zm, zf, out,
    nodes, metv, jacv, face, recv, edge, corner, codes, csem, ssem, rsem, ready,
):
    gx, gz = lax.axis_index("gx"), lax.axis_index("gz")
    x_to = [lax.rem(gx + nx - 1, nx), gx, lax.rem(gx + 1, nx)]
    z_to = [lax.rem(gz + nz - 1, nz), gz, lax.rem(gz + 1, nz)]
    sides = [(1, 0), (-1, 0), (0, 1), (0, -1)]
    diagonals = [(1, 1), (1, -1), (-1, 1), (-1, -1)]
    target = lambda way: (x_to[way[0] + 1], z_to[way[1] + 1])

    loads = [(ref, codes.at[n]) for n, ref in enumerate((xm, xf, zm, zf))]
    loads += [(cons_n, nodes), (met_n, metv), (jac_n, jacv)]
    loads = [pltpu.make_async_copy(a, b, csem.at[n]) for n, (a, b) in enumerate(loads)]
    for copy in loads:
        copy.start()

    corner[...] = jnp.zeros_like(corner)
    even = lax.rem(gz, 2) == 0
    barrier = pltpu.get_barrier_semaphore()
    for way in ((1, -1), (-1, -1), (0, -1)):
        pl.semaphore_signal(barrier, inc=1, device_id=target(way), device_id_type=MESH)

    @pl.when(even)
    def _():
        for way in ((1, 0), (-1, 0)):
            pl.semaphore_signal(barrier, inc=1, device_id=target(way), device_id_type=MESH)

    pl.semaphore_wait(barrier, 5 - 2 * lax.rem(gz, 2))
    for way in ((1, 1), (-1, 1), (0, 1)):
        pl.semaphore_signal(ready, inc=1, device_id=target(way), device_id_type=MESH)

    low, up = pl.ds(0, 4), pl.ds(4, 4)
    sub = lax.broadcasted_iota(jnp.int32, (8, 128), 0)
    lane = lax.broadcasted_iota(jnp.int32, (8, 128), 1)
    row, col = sub & 3, lane & 3
    lower = sub < 4
    half = sub >> 2
    side = jnp.where(lower, -1.0, 1.0)
    x_node = [jnp.where(lower, 1.0, 0.0), jnp.where(lower, 0.0, 1.0)]
    z_edge = jnp.where((row == 0) | (row == 3), 1.0, 0.0)
    cross_index = half * 3 + jnp.where(row == 3, 4, 0)
    z_index = half + jnp.where(row == 3, 4, 0)
    z_from = ((sub & 1) << 2) + half * 3
    z_first = row < 2
    cz = [pick(row, [weak[a, a ^ s] for a in range(4)]) for s in range(4)]
    cy = [pick(col, [weak[a, a ^ s] for a in range(4)]) for s in range(4)]
    cx = [
        [
            [
                jnp.where(lower, float(weak[2 * v, 2 * w + s]), float(weak[2 * v + 1, 2 * w + 1 - s]))
                for s in range(2)
            ]
            for w in range(2)
        ]
        for v in range(2)
    ]
    wall = (lane == 0) | (lane == 127)
    wall_sign = jnp.where(wall, -1.0, 1.0)
    y_other = jnp.where(
        wall, lane, jnp.where(col == 0, lane - 1, jnp.where(col == 3, lane + 1, lane))
    )
    y_lead = jnp.where((col == 0) & (lane > 0), lane - 1, lane)
    y_side = jnp.where(col == 0, -3.0, jnp.where(col == 3, 3.0, 0.0))
    y_jump = jnp.abs(y_side)
    edge_side = jnp.where(row == 0, -3.0, jnp.where(row == 3, 3.0, 0.0))

    def d_x(v):
        r = jnp.stack([pltpu.roll(v[n], 4, 1) for n in range(v.shape[0])])
        parts = [
            cx[n][0][0] * v[:, 0] + cx[n][0][1] * r[:, 0] + cx[n][1][0] * v[:, 1] + cx[n][1][1] * r[:, 1]
            for n in range(2)
        ]
        return jnp.stack(parts, 1)

    def d_z(v):
        result = cz[0] * v
        for s in range(1, 4):
            result = result + cz[s] * along(v, sub ^ s, 0)
        return result

    def d_y(v):
        result = cy[0] * v
        for s in range(1, 4):
            result = result + cy[s] * along(v, lane ^ s, 1)
        return result

    def to_faces(v):
        ends = along(v, z_from, 0)
        return jnp.stack([jnp.where(lower, v[0], v[1]), jnp.where(z_first, ends[0], ends[1])])

    def to_nodes(f):
        z0 = along(f[1], z_index, 0)
        z1 = along(f[1], z_index + 2, 0)
        return jnp.stack([f[0] * x_node[0] + z0 * z_edge, f[0] * x_node[1] + z1 * z_edge])

    def crossed(f):
        return along(f, cross_index, 0)

    for copy in loads[:4]:
        copy.wait()
    lead, lead_edge, lane_one, row_in, row_out, lane_three = [], [], [], [], [], []
    rows_at = lax.broadcasted_iota(jnp.int32, (8, 32), 0)
    for axis in range(2):
        word = codes[2 * axis + 1] + 8 * codes[2 * axis]
        first = jnp.broadcast_to(word[0:1], (8, 32))
        second = jnp.broadcast_to(word[1:2], (8, 32))
        cross = jnp.where((rows_at & 3) < 2, first, second)
        word = jnp.where(rows_at < 4, first, second)
        cross = along(jnp.concatenate([cross] * 4, 1), lane >> 2, 1)
        word = along(jnp.concatenate([word] * 4, 1), lane >> 2, 1)
        first, second = (word & 1) * 3, ((word >> 1) & 1) * 3
        swap = (word & 4) != 0
        lead.append(word >> 3)
        lead_edge.append(cross >> 3)
        lane_one.append(lane ^ jnp.where(swap, row ^ first ^ second, second))
        row_in.append(sub ^ jnp.where(swap, col ^ jnp.where(lower, first, second), first))
        row_out.append(sub ^ jnp.where(swap, col ^ jnp.where(lower, second, first), first))
        lane_three.append(lane ^ jnp.where(swap, row, 0))
    lead = jnp.stack(lead).astype(jnp.float32)
    leads = lead > 0.5
    lead_edge = jnp.stack(lead_edge[::-1]).astype(jnp.float32)

    def orient(layers, row_two):
        parts = []
        for axis in range(2):
            layer = along(layers[axis], lane_one[axis], 1)
            layer = along(layer, row_two[axis], 0)
            parts.append(along(layer, lane_three[axis], 1))
        return jnp.stack(parts)

    loads[4].wait()
    state = [nodes[k] for k in range(5)]
    velocity, pressure, warm = primitives(state)
    lifted = jnp.stack(velocity + [warm])
    own_velocity = [to_faces(v) for v in velocity]
    own_warm = to_faces(warm)
    own_lifted = own_velocity + [own_warm]
    loads[5].wait()
    metric = [[metv[g, d] for d in range(3)] for g in range(3)]
    own_row = [
        jnp.stack([to_faces(metric[0][d])[0], to_faces(metric[1][d])[1]]) for d in range(3)
    ]
    seen = [orient(v, row_out) for v in own_lifted + [lead * own_row[d] for d in range(3)]]
    for k in range(7):
        edge[0, k] = crossed(seen[k][0])
        edge[1, k] = seen[k][1]

    corner_sends = []
    for n, way in enumerate(diagonals):
        at = (3 if way[0] > 0 else 0) + (4 if way[1] > 0 else 0)
        corner_sends.append(
            pltpu.make_async_remote_copy(
                src_ref=edge.at[:, :, pl.ds(at, 1)],
                dst_ref=corner.at[:, :, pl.ds(7 - at, 1)],
                send_sem=ssem.at[4 + n],
                recv_sem=rsem.at[4 + n],
                device_id=target(way),
                device_id_type=MESH,
            )
        )
    corner_sends[0].start()
    corner_sends[2].start()

    def products(g):
        return (lifted[:, None] * jnp.stack(metric[g])[None]).reshape(12, 2, 8, 128)

    partial = d_x(products(0)) + d_z(products(1)) + d_y(products(2))
    y_normal = [along(metric[2][d], y_lead, 1) for d in range(3)]
    y_sums = [
        y_side * (lifted[k] + (wall_sign if k < 3 else 1.0) * along(lifted[k], y_other, 1))
        for k in range(4)
    ]
    loads[6].wait()
    inverse_j = 1.0 / jacv[...]
    scaled = visc_coef * inverse_j
    partial = [
        [scaled * (partial[3 * k + d] + y_sums[k] * y_normal[d]) for d in range(3)]
        for k in range(4)
    ]
    face_partial = [[to_faces(partial[k][d]) for d in range(3)] for k in range(4)]
    face_scaled = to_faces(scaled)
    own = [to_faces(state[k]) for k in range(5)]
    for k in range(5):
        face[:, k] = own[k]
    for d in range(3):
        face[:, 5 + d] = own_row[d]
    for k in range(4):
        for d in range(3):
            face[:, 8 + 3 * k + d] = face_partial[k][d]
    face[:, 20] = face_scaled
    for d in range(3):
        across = to_faces(metric[1][d])[0], to_faces(metric[0][d])[1]
        face[:, 21 + d] = lead_edge * jnp.stack(across)

    sends = []
    for n, way in enumerate(sides):
        axis, from_up = n // 2, n % 2 == 0
        sends.append(
            pltpu.make_async_remote_copy(
                src_ref=face.at[axis, :, up if from_up else low],
                dst_ref=recv.at[axis, :, low if from_up else up],
                send_sem=ssem.at[n],
                recv_sem=rsem.at[n],
                device_id=target(way),
                device_id_type=MESH,
            )
        )
    sends[2].start()

    @pl.when(even)
    def _():
        sends[0].start()
        sends[1].start()

    pl.semaphore_wait(ready, 3)
    corner_sends[1].start()
    corner_sends[3].start()
    sends[3].start()

    @pl.when(jnp.logical_not(even))
    def _():
        sends[0].start()
        sends[1].start()

    inviscid = flows(state, velocity, pressure)
    own_inviscid = flows(own, own_velocity, to_faces(pressure))
    own_sound = jnp.sqrt(gamma_gas * own_warm)
    size_y = jnp.sqrt(dot3(y_normal, y_normal))
    speed = wave(velocity, jnp.sqrt(gamma_gas * warm), y_normal, size_y)
    speed = y_jump * jnp.maximum(speed, along(speed, y_other, 1))
    y_terms = []
    for k in range(5):
        sign = wall_sign if 1 <= k <= 3 else 1.0
        y_terms.append(speed * (state[k] - sign * along(state[k], y_other, 1)))
    mass_y = dot3(state[1:4], y_normal)
    mass_terms = y_terms[0] + y_side * (mass_y + wall_sign * along(mass_y, y_other, 1))
    mass_flux = [dot3(state[1:4], metric[g])[None] for g in range(3)]
    mass_terms = mass_terms + (d_x(mass_flux[0]) + d_z(mass_flux[1]) + d_y(mass_flux[2]))[0]
    mass_terms = -inverse_j * mass_terms

    for copy in sends:
        copy.wait_recv()

    they = [recv[:, k] for k in range(8)]
    they_scaled = recv[:, 20]
    they_velocity, they_pressure, they_warm = primitives(they)
    they_lifted = they_velocity + [they_warm]
    they_normal = [jnp.where(leads, seen[4 + d], they[5 + d]) for d in range(3)]
    they_sums = [(-3.0 * side) * (they_lifted[k] + seen[k]) for k in range(4)]
    they_slopes = [
        [
            recv[:, 8 + 3 * k + d]
            + (they_scaled * they_sums[k]) * they_normal[d]
            for d in range(3)
        ]
        for k in range(4)
    ]
    they_inviscid = flows(they, they_velocity, they_pressure)
    moment, energy = fluxes(they_inviscid, they_velocity, they_slopes)
    they_half = [dot3(they[1:4], they_normal)]
    they_half += [dot3(moment[j], they_normal) for j in range(3)]
    they_half += [dot3(energy, they_normal)]
    they_size = jnp.sqrt(dot3(they_normal, they_normal))
    they_speed = wave(they_velocity, jnp.sqrt(gamma_gas * they_warm), they_normal, they_size)

    other = [orient(they[k], row_in) for k in range(5)]
    other_half = [orient(they_half[k], row_in) for k in range(5)]
    other_speed = orient(they_speed, row_in)
    sums = [-orient(they_sums[k], row_in) for k in range(4)]
    normal = [jnp.where(leads, own_row[d], orient(they[5 + d], row_in)) for d in range(3)]

    def both_crossed(f):
        return jnp.stack([crossed(f[1]), crossed(f[0])])

    cross_sums = [z_edge * both_crossed(sums[k]) for k in range(4)]
    cross_normal = [both_crossed(normal[d]) for d in range(3)]
    face_slopes = [
        [
            face_partial[k][d]
            + face_scaled * (sums[k] * normal[d] + cross_sums[k] * cross_normal[d])
            for d in range(3)
        ]
        for k in range(4)
    ]
    moment, energy = fluxes(own_inviscid, own_velocity, face_slopes)
    own_half = [dot3(own[1:4], normal)]
    own_half += [dot3(moment[j], normal) for j in range(3)] + [dot3(energy, normal)]
    own_speed = wave(own_velocity, own_sound, normal, jnp.sqrt(dot3(normal, normal)))
    speed = 3.0 * jnp.maximum(own_speed, other_speed)
    tile_terms = [
        (3.0 * side) * (own_half[k] + other_half[k]) - speed * (other[k] - own[k])
        for k in range(5)
    ]

    z_sums = [jnp.stack([along(sums[k][1], z_index, 0), along(sums[k][1], z_index + 2, 0)]) * z_edge for k in range(4)]
    z_normal = [jnp.stack([along(normal[d][1], z_index, 0), along(normal[d][1], z_index + 2, 0)]) for d in range(3)]
    x_mask = jnp.stack(x_node)
    slopes = [
        [
            partial[k][d]
            + scaled * (x_mask * (sums[k][0] * normal[d][0]) + z_sums[k] * z_normal[d])
            for d in range(3)
        ]
        for k in range(4)
    ]
    moment, energy = fluxes(inviscid, velocity, slopes)

    def through(rows):
        return [dot3(moment[j], rows) for j in range(3)] + [dot3(energy, rows)]

    total = d_x(jnp.stack(through(metric[0])))
    total = total + d_z(jnp.stack(through(metric[1])))
    total = total + d_y(jnp.stack(through(metric[2])))

    half_y = through(y_normal)
    heat_y = (-2.0 * heat_ratio) * dot3(slopes[3], y_normal)
    for k in range(4):
        both = half_y[k] + along(half_y[k], y_other, 1)
        if k == 3:
            both = jnp.where(wall, heat_y, both)
        y_terms[1 + k] = y_terms[1 + k] + y_side * both
    out[0] = mass_terms - inverse_j * to_nodes(tile_terms[0])
    ready = [
        -inverse_j * (total[k] + y_terms[1 + k] + to_nodes(tile_terms[1 + k])) for k in range(4)
    ]

    for copy in corner_sends:
        copy.wait_recv()
    line = [jnp.stack([crossed(corner[1, k]), corner[0, k]]) for k in range(7)]
    line_sums = [
        (edge_side * they_scaled) * (they_lifted[k] + line[k]) for k in range(4)
    ]
    line_normal = [recv[:, 21 + d] + line[4 + d] for d in range(3)]
    onto = dot3(line_normal, they_normal)
    carried = dot3(line_sums, they_normal)
    spread = (2.0 / 3.0) * dot3(line_sums, line_normal)
    drag = [
        spread * they_normal[j] - line_sums[j] * onto - line_normal[j] * carried
        for j in range(3)
    ]
    drag.append(dot3(they_velocity, drag) - heat_ratio * (line_sums[3] * onto))
    for k in range(4):
        late = (3.0 * side) * orient(drag[k], row_in)
        out[1 + k] = ready[k] - inverse_j * to_nodes(late)
    for copy in sends + corner_sends:
        copy.wait_send()


def local(nx, nz, conserved, jacobian, metric, x_master, x_flip, z_master, z_flip):
    anywhere = pl.BlockSpec(memory_space=pl.ANY)
    words = [v.reshape(2, 32) for v in (x_master, x_flip, z_master, z_flip)]
    result = pl.pallas_call(
        functools.partial(kernel, nx, nz),
        out_shape=pltpu.VMEM((5, 2, 8, 128), jnp.float32),
        in_specs=[anywhere] * 7,
        out_specs=pl.BlockSpec(memory_space=pltpu.VMEM),
        scratch_shapes=[
            pltpu.VMEM((5, 2, 8, 128), jnp.float32),
            pltpu.VMEM((3, 3, 2, 8, 128), jnp.float32),
            pltpu.VMEM((2, 8, 128), jnp.float32),
            pltpu.VMEM((2, 24, 8, 128), jnp.float32),
            pltpu.VMEM((2, 24, 8, 128), jnp.float32),
            pltpu.VMEM((2, 7, 8, 128), jnp.float32),
            pltpu.VMEM((2, 7, 8, 128), jnp.float32),
            pltpu.VMEM((4, 2, 32), jnp.int32),
            pltpu.SemaphoreType.DMA((7,)),
            pltpu.SemaphoreType.DMA((8,)),
            pltpu.SemaphoreType.DMA((8,)),
            pltpu.SemaphoreType.REGULAR,
        ],
        compiler_params=pltpu.CompilerParams(collective_id=0, has_side_effects=True),
    )(
        conserved.reshape(5, 2, 8, 128),
        metric.reshape(3, 3, 2, 8, 128),
        jacobian.reshape(2, 8, 128),
        *words,
    )
    return result.reshape(5, 4, 4, 128)


def solution(mesh):
    flags = P("gx", "gz", None)
    in_specs = (P(None, "gx", "gz", None), flags, P(None, None, "gx", "gz", None)) + (flags,) * 4
    return jax.shard_map(
        functools.partial(local, mesh.shape["gx"], mesh.shape["gz"]),
        mesh=mesh,
        in_specs=in_specs,
        out_specs=P(None, "gx", "gz", None),
        check_vma=False,
    )
```

```python
import functools
import math

import jax
import jax.numpy as jnp
import numpy as np
from jax import lax
from jax.experimental import pallas as pl
from jax.experimental.pallas import tpu as pltpu
from jax.sharding import PartitionSpec as P

MESH = pl.DeviceIdType.MESH
gamma_gas = 1.4
visc_coef = 0.1
prandtl = 0.72
heat_ratio = gamma_gas / ((gamma_gas - 1.0) * prandtl)


def node_table():
    points = np.array([-1.0, -math.sqrt(0.2), math.sqrt(0.2), 1.0])
    scales = np.array(
        [np.prod([points[r] - points[s] for s in range(4) if s != r]) for r in range(4)]
    )
    table = np.zeros((4, 4))
    for r in range(4):
        for c in range(4):
            if r != c:
                table[r, c] = scales[r] / (scales[c] * (points[r] - points[c]))
        table[r, r] = -np.sum(table[r])
    return table


weak = node_table()
weak[0, 0] += 6.0
weak[3, 3] -= 6.0


def pick(index, values):
    result = jnp.full(index.shape, float(values[3]), jnp.float32)
    for at in range(3):
        result = jnp.where(index == at, float(values[at]), result)
    return result


def along(values, index, axis):
    shape = values.shape
    flat = values.reshape((-1, 8, 128))
    parts = [
        jnp.take_along_axis(flat[n], index, axis=axis, mode="promise_in_bounds")
        for n in range(flat.shape[0])
    ]
    return jnp.stack(parts).reshape(shape)


def primitives(state):
    inverse = 1.0 / state[0]
    velocity = [state[1 + j] * inverse for j in range(3)]
    kinetic = state[1] * velocity[0] + state[2] * velocity[1] + state[3] * velocity[2]
    pressure = (gamma_gas - 1.0) * (state[4] - 0.5 * kinetic)
    return velocity, pressure, pressure * inverse


def dot3(left, right):
    return left[0] * right[0] + left[1] * right[1] + left[2] * right[2]


def flows(state, velocity, pressure):
    moment = [[None] * 3 for _ in range(3)]
    for j in range(3):
        for d in range(j, 3):
            flow = state[1 + j] * velocity[d]
            moment[j][d] = moment[d][j] = flow + pressure if j == d else flow
    total = state[4] + pressure
    return moment, [total * velocity[d] for d in range(3)]


def fluxes(inviscid, velocity, slopes):
    third = (2.0 / 3.0) * (slopes[0][0] + slopes[1][1] + slopes[2][2])
    stress = [[None] * 3 for _ in range(3)]
    moment = [[None] * 3 for _ in range(3)]
    for j in range(3):
        for d in range(j, 3):
            tau = slopes[j][d] + slopes[d][j]
            if j == d:
                tau = tau - third
            stress[j][d] = stress[d][j] = tau
            moment[j][d] = moment[d][j] = inviscid[0][j][d] - tau
    energy = [
        inviscid[1][d] - dot3(velocity, stress[d]) - heat_ratio * slopes[3][d]
        for d in range(3)
    ]
    return moment, energy


def wave(velocity, sound, normal, size):
    return jnp.abs(dot3(velocity, normal)) + sound * size


def kernel(
    nx, nz, cons_n, met_n, jac_n, cons_f, met_f, xm, xf, zm, zf, out,
    nodes, metv, jacv, face, recv, corner, words, theirs, codes, csem, ssem, rsem, ready,
):
    gx, gz = lax.axis_index("gx"), lax.axis_index("gz")
    x_to = [lax.rem(gx + nx - 1, nx), gx, lax.rem(gx + 1, nx)]
    z_to = [lax.rem(gz + nz - 1, nz), gz, lax.rem(gz + 1, nz)]
    sides = [(1, 0), (-1, 0), (0, 1), (0, -1)]
    diagonals = [(1, 1), (1, -1), (-1, 1), (-1, -1)]
    target = lambda way: (x_to[way[0] + 1], z_to[way[1] + 1])

    even = lax.rem(gz, 2) == 0
    barrier = pltpu.get_barrier_semaphore()
    for way in ((1, -1), (-1, -1), (0, -1)):
        pl.semaphore_signal(barrier, inc=1, device_id=target(way), device_id_type=MESH)

    @pl.when(even)
    def _():
        for way in ((1, 0), (-1, 0)):
            pl.semaphore_signal(barrier, inc=1, device_id=target(way), device_id_type=MESH)

    pl.semaphore_wait(barrier, 5 - 2 * lax.rem(gz, 2))
    for way in ((1, 1), (-1, 1), (0, 1)):
        pl.semaphore_signal(ready, inc=1, device_id=target(way), device_id_type=MESH)

    low, up = pl.ds(0, 4), pl.ds(4, 4)
    five, three = pl.ds(0, 5), pl.ds(5, 3)
    corner_sends = []
    for n, way in enumerate(diagonals):
        x_at, z_at = (3 if way[0] > 0 else 0), (3 if way[1] > 0 else 0)
        x_from, z_from_ = (0 if way[0] > 0 else 1), (0 if way[1] > 0 else 1)
        x_rows, z_rows = (low, up)[x_from], (low, up)[z_from_]
        pairs = [
            (cons_f.at[:, :, z_at, :], corner.at[0, x_from, five, z_rows]),
            (met_f.at[1, :, :, z_at, :], corner.at[0, x_from, three, z_rows]),
            (cons_f.at[:, x_at], corner.at[1, z_from_, five, x_rows]),
            (met_f.at[0, :, x_at], corner.at[1, z_from_, three, x_rows]),
        ]
        for m, (source, place) in enumerate(pairs):
            corner_sends.append(
                pltpu.make_async_remote_copy(
                    src_ref=source,
                    dst_ref=place,
                    send_sem=ssem.at[8 + 4 * n + m],
                    recv_sem=rsem.at[8 + 4 * n + m],
                    device_id=target(way),
                    device_id_type=MESH,
                )
            )
    corner_next = corner_sends[0:4] + corner_sends[8:12]
    corner_previous = corner_sends[4:8] + corner_sends[12:16]
    for copy in corner_next:
        copy.start()

    loads = [(ref, codes.at[n]) for n, ref in enumerate((xm, xf, zm, zf))]
    loads += [(cons_n, nodes), (met_n, metv), (jac_n, jacv)]
    loads = [pltpu.make_async_copy(a, b, csem.at[n]) for n, (a, b) in enumerate(loads)]
    for copy in loads:
        copy.start()

    sub = lax.broadcasted_iota(jnp.int32, (8, 128), 0)
    lane = lax.broadcasted_iota(jnp.int32, (8, 128), 1)
    row, col = sub & 3, lane & 3
    lower = sub < 4
    half = sub >> 2
    side = jnp.where(lower, -1.0, 1.0)
    x_node = [jnp.where(lower, 1.0, 0.0), jnp.where(lower, 0.0, 1.0)]
    z_edge = jnp.where((row == 0) | (row == 3), 1.0, 0.0)
    cross_index = half * 3 + jnp.where(row == 3, 4, 0)
    z_index = half + jnp.where(row == 3, 4, 0)
    z_from = ((sub & 1) << 2) + half * 3
    z_first = row < 2
    cz = [pick(row, [weak[a, a ^ s] for a in range(4)]) for s in range(4)]
    cy = [pick(col, [weak[a, a ^ s] for a in range(4)]) for s in range(4)]
    cx = [
        [
            [
                jnp.where(lower, float(weak[2 * v, 2 * w + s]), float(weak[2 * v + 1, 2 * w + 1 - s]))
                for s in range(2)
            ]
            for w in range(2)
        ]
        for v in range(2)
    ]
    wall = (lane == 0) | (lane == 127)
    wall_sign = jnp.where(wall, -1.0, 1.0)
    y_other = jnp.where(
        wall, lane, jnp.where(col == 0, lane - 1, jnp.where(col == 3, lane + 1, lane))
    )
    y_lead = jnp.where((col == 0) & (lane > 0), lane - 1, lane)
    y_side = jnp.where(col == 0, -3.0, jnp.where(col == 3, 3.0, 0.0))
    y_jump = jnp.abs(y_side)
    edge_side = jnp.where(row == 0, -3.0, jnp.where(row == 3, 3.0, 0.0))

    def d_x(v):
        r = jnp.stack([pltpu.roll(v[n], 4, 1) for n in range(v.shape[0])])
        parts = [
            cx[n][0][0] * v[:, 0] + cx[n][0][1] * r[:, 0] + cx[n][1][0] * v[:, 1] + cx[n][1][1] * r[:, 1]
            for n in range(2)
        ]
        return jnp.stack(parts, 1)

    def d_z(v):
        result = cz[0] * v
        for s in range(1, 4):
            result = result + cz[s] * along(v, sub ^ s, 0)
        return result

    def d_y(v):
        result = cy[0] * v
        for s in range(1, 4):
            result = result + cy[s] * along(v, lane ^ s, 1)
        return result

    def to_faces(v):
        ends = along(v, z_from, 0)
        return jnp.stack([jnp.where(lower, v[0], v[1]), jnp.where(z_first, ends[0], ends[1])])

    def to_nodes(f):
        z0 = along(f[1], z_index, 0)
        z1 = along(f[1], z_index + 2, 0)
        return jnp.stack([f[0] * x_node[0] + z0 * z_edge, f[0] * x_node[1] + z1 * z_edge])

    def crossed(f):
        return along(f, cross_index, 0)

    for copy in loads[:4]:
        copy.wait()
    lead, lead_edge, lane_one, row_in, row_out, lane_three = [], [], [], [], [], []
    rows_at = lax.broadcasted_iota(jnp.int32, (8, 32), 0)
    for axis in range(2):
        word = codes[2 * axis + 1] + 8 * codes[2 * axis]
        first = jnp.broadcast_to(word[0:1], (8, 32))
        second = jnp.broadcast_to(word[1:2], (8, 32))
        cross = jnp.where((rows_at & 3) < 2, first, second)
        word = jnp.where(rows_at < 4, first, second)
        cross = along(jnp.concatenate([cross] * 4, 1), lane >> 2, 1)
        word = along(jnp.concatenate([word] * 4, 1), lane >> 2, 1)
        first, second = (word & 1) * 3, ((word >> 1) & 1) * 3
        swap = (word & 4) != 0
        words[axis] = word
        lead.append(word >> 3)
        lead_edge.append(cross >> 3)
        lane_one.append(lane ^ jnp.where(swap, row ^ first ^ second, second))
        row_in.append(sub ^ jnp.where(swap, col ^ jnp.where(lower, first, second), first))
        row_out.append(sub ^ jnp.where(swap, col ^ jnp.where(lower, second, first), first))
        lane_three.append(lane ^ jnp.where(swap, row, 0))
    lead = jnp.stack(lead).astype(jnp.float32)
    leads = lead > 0.5
    lead_edge = jnp.stack(lead_edge[::-1]).astype(jnp.float32)

    def orient(layers, row_two):
        parts = []
        for axis in range(2):
            layer = along(layers[axis], lane_one[axis], 1)
            layer = along(layer, row_two[axis], 0)
            parts.append(along(layer, lane_three[axis], 1))
        return jnp.stack(parts)

    loads[4].wait()
    state = [nodes[k] for k in range(5)]
    velocity, pressure, warm = primitives(state)
    lifted = jnp.stack(velocity + [warm])
    own_velocity = [to_faces(v) for v in velocity]
    own_warm = to_faces(warm)
    own_lifted = own_velocity + [own_warm]
    loads[5].wait()
    metric = [[metv[g, d] for d in range(3)] for g in range(3)]
    own_row = [
        jnp.stack([to_faces(metric[0][d])[0], to_faces(metric[1][d])[1]]) for d in range(3)
    ]
    seen = [orient(v, row_out) for v in own_lifted + [lead * own_row[d] for d in range(3)]]
    def products(g):
        return (lifted[:, None] * jnp.stack(metric[g])[None]).reshape(12, 2, 8, 128)

    partial = d_x(products(0)) + d_z(products(1)) + d_y(products(2))
    y_normal = [along(metric[2][d], y_lead, 1) for d in range(3)]
    y_sums = [
        y_side * (lifted[k] + (wall_sign if k < 3 else 1.0) * along(lifted[k], y_other, 1))
        for k in range(4)
    ]
    loads[6].wait()
    inverse_j = 1.0 / jacv[...]
    scaled = visc_coef * inverse_j
    partial = [
        [scaled * (partial[3 * k + d] + y_sums[k] * y_normal[d]) for d in range(3)]
        for k in range(4)
    ]
    face_partial = [[to_faces(partial[k][d]) for d in range(3)] for k in range(4)]
    face_scaled = to_faces(scaled)
    own = [to_faces(state[k]) for k in range(5)]
    for k in range(5):
        face[:, k] = own[k]
    for d in range(3):
        face[:, 5 + d] = own_row[d]
    for k in range(4):
        for d in range(3):
            face[:, 8 + 3 * k + d] = face_partial[k][d]
    face[:, 20] = face_scaled
    for d in range(3):
        across = to_faces(metric[1][d])[0], to_faces(metric[0][d])[1]
        face[:, 21 + d] = lead_edge * jnp.stack(across)

    sends = []
    for n, way in enumerate(sides):
        axis, from_up = n // 2, n % 2 == 0
        sends.append(
            pltpu.make_async_remote_copy(
                src_ref=face.at[axis, :, up if from_up else low],
                dst_ref=recv.at[axis, :, low if from_up else up],
                send_sem=ssem.at[n],
                recv_sem=rsem.at[n],
                device_id=target(way),
                device_id_type=MESH,
            )
        )
        sends.append(
            pltpu.make_async_remote_copy(
                src_ref=words.at[1 - axis],
                dst_ref=theirs.at[axis, 0 if from_up else 1],
                send_sem=ssem.at[4 + n],
                recv_sem=rsem.at[4 + n],
                device_id=target(way),
                device_id_type=MESH,
            )
        )
    for copy in sends[4:6]:
        copy.start()

    @pl.when(even)
    def _():
        for copy in sends[0:4]:
            copy.start()

    pl.semaphore_wait(ready, 3)
    for copy in corner_previous + sends[6:8]:
        copy.start()

    @pl.when(jnp.logical_not(even))
    def _():
        for copy in sends[0:4]:
            copy.start()

    inviscid = flows(state, velocity, pressure)
    own_inviscid = flows(own, own_velocity, to_faces(pressure))
    own_sound = jnp.sqrt(gamma_gas * own_warm)
    size_y = jnp.sqrt(dot3(y_normal, y_normal))
    speed = wave(velocity, jnp.sqrt(gamma_gas * warm), y_normal, size_y)
    speed = y_jump * jnp.maximum(speed, along(speed, y_other, 1))
    y_terms = []
    for k in range(5):
        sign = wall_sign if 1 <= k <= 3 else 1.0
        y_terms.append(speed * (state[k] - sign * along(state[k], y_other, 1)))
    mass_y = dot3(state[1:4], y_normal)
    mass_terms = y_terms[0] + y_side * (mass_y + wall_sign * along(mass_y, y_other, 1))
    mass_flux = [dot3(state[1:4], metric[g])[None] for g in range(3)]
    mass_terms = mass_terms + (d_x(mass_flux[0]) + d_z(mass_flux[1]) + d_y(mass_flux[2]))[0]
    mass_terms = -inverse_j * mass_terms

    for copy in sends:
        copy.wait_recv()

    they = [recv[:, k] for k in range(8)]
    they_scaled = recv[:, 20]
    they_velocity, they_pressure, they_warm = primitives(they)
    they_lifted = they_velocity + [they_warm]
    they_normal = [jnp.where(leads, seen[4 + d], they[5 + d]) for d in range(3)]
    they_sums = [(-3.0 * side) * (they_lifted[k] + seen[k]) for k in range(4)]
    they_slopes = [
        [
            recv[:, 8 + 3 * k + d]
            + (they_scaled * they_sums[k]) * they_normal[d]
            for d in range(3)
        ]
        for k in range(4)
    ]
    they_inviscid = flows(they, they_velocity, they_pressure)
    moment, energy = fluxes(they_inviscid, they_velocity, they_slopes)
    they_half = [dot3(they[1:4], they_normal)]
    they_half += [dot3(moment[j], they_normal) for j in range(3)]
    they_half += [dot3(energy, they_normal)]
    they_size = jnp.sqrt(dot3(they_normal, they_normal))
    they_speed = wave(they_velocity, jnp.sqrt(gamma_gas * they_warm), they_normal, they_size)

    other = [orient(they[k], row_in) for k in range(5)]
    other_half = [orient(they_half[k], row_in) for k in range(5)]
    other_speed = orient(they_speed, row_in)
    sums = [-orient(they_sums[k], row_in) for k in range(4)]
    normal = [jnp.where(leads, own_row[d], orient(they[5 + d], row_in)) for d in range(3)]

    def both_crossed(f):
        return jnp.stack([crossed(f[1]), crossed(f[0])])

    cross_sums = [z_edge * both_crossed(sums[k]) for k in range(4)]
    cross_normal = [both_crossed(normal[d]) for d in range(3)]
    face_slopes = [
        [
            face_partial[k][d]
            + face_scaled * (sums[k] * normal[d] + cross_sums[k] * cross_normal[d])
            for d in range(3)
        ]
        for k in range(4)
    ]
    moment, energy = fluxes(own_inviscid, own_velocity, face_slopes)
    own_half = [dot3(own[1:4], normal)]
    own_half += [dot3(moment[j], normal) for j in range(3)] + [dot3(energy, normal)]
    own_speed = wave(own_velocity, own_sound, normal, jnp.sqrt(dot3(normal, normal)))
    speed = 3.0 * jnp.maximum(own_speed, other_speed)
    tile_terms = [
        (3.0 * side) * (own_half[k] + other_half[k]) - speed * (other[k] - own[k])
        for k in range(5)
    ]

    z_sums = [jnp.stack([along(sums[k][1], z_index, 0), along(sums[k][1], z_index + 2, 0)]) * z_edge for k in range(4)]
    z_normal = [jnp.stack([along(normal[d][1], z_index, 0), along(normal[d][1], z_index + 2, 0)]) for d in range(3)]
    x_mask = jnp.stack(x_node)
    slopes = [
        [
            partial[k][d]
            + scaled * (x_mask * (sums[k][0] * normal[d][0]) + z_sums[k] * z_normal[d])
            for d in range(3)
        ]
        for k in range(4)
    ]
    moment, energy = fluxes(inviscid, velocity, slopes)

    def through(rows):
        return [dot3(moment[j], rows) for j in range(3)] + [dot3(energy, rows)]

    total = d_x(jnp.stack(through(metric[0])))
    total = total + d_z(jnp.stack(through(metric[1])))
    total = total + d_y(jnp.stack(through(metric[2])))

    half_y = through(y_normal)
    heat_y = (-2.0 * heat_ratio) * dot3(slopes[3], y_normal)
    for k in range(4):
        both = half_y[k] + along(half_y[k], y_other, 1)
        if k == 3:
            both = jnp.where(wall, heat_y, both)
        y_terms[1 + k] = y_terms[1 + k] + y_side * both
    out[0] = mass_terms - inverse_j * to_nodes(tile_terms[0])
    ready = [
        -inverse_j * (total[k] + y_terms[1 + k] + to_nodes(tile_terms[1 + k])) for k in range(4)
    ]

    wanted = jnp.where(lower, jnp.where(row == 3, 7, 3), jnp.where(row == 3, 4, 0))
    turn_one, turn_row, turn_three, turn_mask = [], [], [], []
    for axis in range(2):
        ones, rows, swaps, masks = [], [], [], []
        for h in range(2):
            word = theirs[axis, h]
            first, second = (word & 1) * 3, ((word >> 1) & 1) * 3
            ones.append(lane ^ jnp.where((word & 4) != 0, row ^ first ^ second, second))
            word = along(word, wanted, 0)
            first, second = (word & 1) * 3, ((word >> 1) & 1) * 3
            swap = (word & 4) != 0
            turned = col ^ jnp.where(wanted < 4, first, second)
            rows.append(wanted ^ jnp.where(swap, turned, first))
            swaps.append(jnp.where(swap, wanted & 3, 0))
            masks.append(1 - (word >> 3))
        turn_one.append(ones)
        turn_row.append(rows)
        turn_three.append(lane ^ jnp.where(lower, swaps[0], swaps[1]))
        turn_mask.append(jnp.where(lower, masks[0], masks[1]).astype(jnp.float32))
    turn_mask = jnp.stack(turn_mask)

    for copy in corner_sends:
        copy.wait_recv()
    met = [[] for _ in range(8)]
    for axis in range(2):
        for k in range(8):
            parts = [
                along(along(corner[axis, h, k], turn_one[axis][h], 1), turn_row[axis][h], 0)
                for h in range(2)
            ]
            met[k].append(along(jnp.where(lower, parts[0], parts[1]), turn_three[axis], 1))
    met = [jnp.stack(v) for v in met]
    met_velocity, _, met_warm = primitives(met)
    line = met_velocity + [met_warm] + [turn_mask * met[5 + d] for d in range(3)]
    line_sums = [
        (edge_side * they_scaled) * (they_lifted[k] + line[k]) for k in range(4)
    ]
    line_normal = [recv[:, 21 + d] + line[4 + d] for d in range(3)]
    onto = dot3(line_normal, they_normal)
    carried = dot3(line_sums, they_normal)
    spread = (2.0 / 3.0) * dot3(line_sums, line_normal)
    drag = [
        spread * they_normal[j] - line_sums[j] * onto - line_normal[j] * carried
        for j in range(3)
    ]
    drag.append(dot3(they_velocity, drag) - heat_ratio * (line_sums[3] * onto))
    for k in range(4):
        late = (3.0 * side) * orient(drag[k], row_in)
        out[1 + k] = ready[k] - inverse_j * to_nodes(late)
    for copy in sends + corner_sends:
        copy.wait_send()


def local(nx, nz, conserved, jacobian, metric, x_master, x_flip, z_master, z_flip):
    anywhere = pl.BlockSpec(memory_space=pl.ANY)
    words = [v.reshape(2, 32) for v in (x_master, x_flip, z_master, z_flip)]
    result = pl.pallas_call(
        functools.partial(kernel, nx, nz),
        out_shape=pltpu.VMEM((5, 2, 8, 128), jnp.float32),
        in_specs=[anywhere] * 9,
        out_specs=pl.BlockSpec(memory_space=pltpu.VMEM),
        scratch_shapes=[
            pltpu.VMEM((5, 2, 8, 128), jnp.float32),
            pltpu.VMEM((3, 3, 2, 8, 128), jnp.float32),
            pltpu.VMEM((2, 8, 128), jnp.float32),
            pltpu.VMEM((2, 24, 8, 128), jnp.float32),
            pltpu.VMEM((2, 24, 8, 128), jnp.float32),
            pltpu.VMEM((2, 2, 8, 8, 128), jnp.float32),
            pltpu.VMEM((2, 8, 128), jnp.int32),
            pltpu.VMEM((2, 2, 8, 128), jnp.int32),
            pltpu.VMEM((4, 2, 32), jnp.int32),
            pltpu.SemaphoreType.DMA((7,)),
            pltpu.SemaphoreType.DMA((24,)),
            pltpu.SemaphoreType.DMA((24,)),
            pltpu.SemaphoreType.REGULAR,
        ],
        compiler_params=pltpu.CompilerParams(collective_id=0, has_side_effects=True),
    )(
        conserved.reshape(5, 2, 8, 128),
        metric.reshape(3, 3, 2, 8, 128),
        jacobian.reshape(2, 8, 128),
        conserved,
        metric,
        *words,
    )
    return result.reshape(5, 4, 4, 128)


def solution(mesh):
    flags = P("gx", "gz", None)
    in_specs = (P(None, "gx", "gz", None), flags, P(None, None, "gx", "gz", None)) + (flags,) * 4
    return jax.shard_map(
        functools.partial(local, mesh.shape["gx"], mesh.shape["gz"]),
        mesh=mesh,
        in_specs=in_specs,
        out_specs=P(None, "gx", "gz", None),
        check_vma=False,
    )
```

```python
import functools
import math

import jax
import jax.numpy as jnp
import numpy as np
from jax import lax
from jax.experimental import pallas as pl
from jax.experimental.pallas import tpu as pltpu
from jax.sharding import PartitionSpec as P

MESH = pl.DeviceIdType.MESH
gamma_gas = 1.4
visc_coef = 0.1
prandtl = 0.72
heat_ratio = gamma_gas / ((gamma_gas - 1.0) * prandtl)


def node_table():
    points = np.array([-1.0, -math.sqrt(0.2), math.sqrt(0.2), 1.0])
    scales = np.array(
        [np.prod([points[r] - points[s] for s in range(4) if s != r]) for r in range(4)]
    )
    table = np.zeros((4, 4))
    for r in range(4):
        for c in range(4):
            if r != c:
                table[r, c] = scales[r] / (scales[c] * (points[r] - points[c]))
        table[r, r] = -np.sum(table[r])
    return table


weak = node_table()
weak[0, 0] += 6.0
weak[3, 3] -= 6.0


def pick(index, values):
    result = jnp.full(index.shape, float(values[3]), jnp.float32)
    for at in range(3):
        result = jnp.where(index == at, float(values[at]), result)
    return result


def along(values, index, axis):
    shape = values.shape
    flat = values.reshape((-1, 8, 128))
    parts = [
        jnp.take_along_axis(flat[n], index, axis=axis, mode="promise_in_bounds")
        for n in range(flat.shape[0])
    ]
    return jnp.stack(parts).reshape(shape)


def primitives(state):
    inverse = 1.0 / state[0]
    velocity = [state[1 + j] * inverse for j in range(3)]
    kinetic = state[1] * velocity[0] + state[2] * velocity[1] + state[3] * velocity[2]
    pressure = (gamma_gas - 1.0) * (state[4] - 0.5 * kinetic)
    return velocity, pressure, pressure * inverse


def dot3(left, right):
    return left[0] * right[0] + left[1] * right[1] + left[2] * right[2]


def flows(state, velocity, pressure):
    moment = [[None] * 3 for _ in range(3)]
    for j in range(3):
        for d in range(j, 3):
            flow = state[1 + j] * velocity[d]
            moment[j][d] = moment[d][j] = flow + pressure if j == d else flow
    total = state[4] + pressure
    return moment, [total * velocity[d] for d in range(3)]


def fluxes(inviscid, velocity, slopes):
    third = (2.0 / 3.0) * (slopes[0][0] + slopes[1][1] + slopes[2][2])
    stress = [[None] * 3 for _ in range(3)]
    moment = [[None] * 3 for _ in range(3)]
    for j in range(3):
        for d in range(j, 3):
            tau = slopes[j][d] + slopes[d][j]
            if j == d:
                tau = tau - third
            stress[j][d] = stress[d][j] = tau
            moment[j][d] = moment[d][j] = inviscid[0][j][d] - tau
    energy = [
        inviscid[1][d] - dot3(velocity, stress[d]) - heat_ratio * slopes[3][d]
        for d in range(3)
    ]
    return moment, energy


def wave(velocity, sound, normal, size):
    return jnp.abs(dot3(velocity, normal)) + sound * size


def kernel(
    nx, nz, cons_n, met_n, jac_n, xm, xf, zm, zf, out,
    nodes, metv, jacv, face, recv, edge, corner, codes, csem, ssem, rsem, ready,
):
    gx, gz = lax.axis_index("gx"), lax.axis_index("gz")
    x_to = [lax.rem(gx + nx - 1, nx), gx, lax.rem(gx + 1, nx)]
    z_to = [lax.rem(gz + nz - 1, nz), gz, lax.rem(gz + 1, nz)]
    sides = [(1, 0), (-1, 0), (0, 1), (0, -1)]
    diagonals = [(1, 1), (1, -1), (-1, 1), (-1, -1)]
    target = lambda way: (x_to[way[0] + 1], z_to[way[1] + 1])

    loads = [(ref, codes.at[n]) for n, ref in enumerate((xm, xf, zm, zf))]
    loads += [(cons_n, nodes), (met_n.at[0:2], metv.at[0:2]), (met_n.at[2], metv.at[2]), (jac_n, jacv)]
    loads = [pltpu.make_async_copy(a, b, csem.at[n]) for n, (a, b) in enumerate(loads)]
    for copy in loads:
        copy.start()

    corner[...] = jnp.zeros_like(corner)
    even = lax.rem(gz, 2) == 0
    barrier = pltpu.get_barrier_semaphore()
    for way in ((1, -1), (-1, -1), (0, -1)):
        pl.semaphore_signal(barrier, inc=1, device_id=target(way), device_id_type=MESH)

    @pl.when(even)
    def _():
        for way in ((1, 0), (-1, 0)):
            pl.semaphore_signal(barrier, inc=1, device_id=target(way), device_id_type=MESH)

    pl.semaphore_wait(barrier, 5 - 2 * lax.rem(gz, 2))
    for way in ((1, 1), (-1, 1), (0, 1)):
        pl.semaphore_signal(ready, inc=1, device_id=target(way), device_id_type=MESH)

    low, up = pl.ds(0, 4), pl.ds(4, 4)
    sub = lax.broadcasted_iota(jnp.int32, (8, 128), 0)
    lane = lax.broadcasted_iota(jnp.int32, (8, 128), 1)
    row, col = sub & 3, lane & 3
    lower = sub < 4
    half = sub >> 2
    side = jnp.where(lower, -1.0, 1.0)
    x_node = [jnp.where(lower, 1.0, 0.0), jnp.where(lower, 0.0, 1.0)]
    z_edge = jnp.where((row == 0) | (row == 3), 1.0, 0.0)
    cross_index = half * 3 + jnp.where(row == 3, 4, 0)
    z_index = half + jnp.where(row == 3, 4, 0)
    z_from = ((sub & 1) << 2) + half * 3
    z_first = row < 2
    cz = [pick(row, [weak[a, a ^ s] for a in range(4)]) for s in range(4)]
    cy = [pick(col, [weak[a, a ^ s] for a in range(4)]) for s in range(4)]
    cx = [
        [
            [
                jnp.where(lower, float(weak[2 * v, 2 * w + s]), float(weak[2 * v + 1, 2 * w + 1 - s]))
                for s in range(2)
            ]
            for w in range(2)
        ]
        for v in range(2)
    ]
    wall = (lane == 0) | (lane == 127)
    wall_sign = jnp.where(wall, -1.0, 1.0)
    y_other = jnp.where(
        wall, lane, jnp.where(col == 0, lane - 1, jnp.where(col == 3, lane + 1, lane))
    )
    y_lead = jnp.where((col == 0) & (lane > 0), lane - 1, lane)
    y_side = jnp.where(col == 0, -3.0, jnp.where(col == 3, 3.0, 0.0))
    y_jump = jnp.abs(y_side)
    edge_side = jnp.where(row == 0, -3.0, jnp.where(row == 3, 3.0, 0.0))

    def d_x(v):
        r = jnp.stack([pltpu.roll(v[n], 4, 1) for n in range(v.shape[0])])
        parts = [
            cx[n][0][0] * v[:, 0] + cx[n][0][1] * r[:, 0] + cx[n][1][0] * v[:, 1] + cx[n][1][1] * r[:, 1]
            for n in range(2)
        ]
        return jnp.stack(parts, 1)

    def d_z(v):
        result = cz[0] * v
        for s in range(1, 4):
            result = result + cz[s] * along(v, sub ^ s, 0)
        return result

    def d_y(v):
        result = cy[0] * v
        for s in range(1, 4):
            result = result + cy[s] * along(v, lane ^ s, 1)
        return result

    def to_faces(v):
        ends = along(v, z_from, 0)
        return jnp.stack([jnp.where(lower, v[0], v[1]), jnp.where(z_first, ends[0], ends[1])])

    def to_nodes(f):
        z0 = along(f[1], z_index, 0)
        z1 = along(f[1], z_index + 2, 0)
        return jnp.stack([f[0] * x_node[0] + z0 * z_edge, f[0] * x_node[1] + z1 * z_edge])

    def crossed(f):
        return along(f, cross_index, 0)

    for copy in loads[:4]:
        copy.wait()
    lead, lead_edge, lane_one, row_in, row_out, lane_three = [], [], [], [], [], []
    rows_at = lax.broadcasted_iota(jnp.int32, (8, 32), 0)
    for axis in range(2):
        word = codes[2 * axis + 1] + 8 * codes[2 * axis]
        first = jnp.broadcast_to(word[0:1], (8, 32))
        second = jnp.broadcast_to(word[1:2], (8, 32))
        cross = jnp.where((rows_at & 3) < 2, first, second)
        word = jnp.where(rows_at < 4, first, second)
        cross = along(jnp.concatenate([cross] * 4, 1), lane >> 2, 1)
        word = along(jnp.concatenate([word] * 4, 1), lane >> 2, 1)
        first, second = (word & 1) * 3, ((word >> 1) & 1) * 3
        swap = (word & 4) != 0
        lead.append(word >> 3)
        lead_edge.append(cross >> 3)
        lane_one.append(lane ^ jnp.where(swap, row ^ first ^ second, second))
        row_in.append(sub ^ jnp.where(swap, col ^ jnp.where(lower, first, second), first))
        row_out.append(sub ^ jnp.where(swap, col ^ jnp.where(lower, second, first), first))
        lane_three.append(lane ^ jnp.where(swap, row, 0))
    lead = jnp.stack(lead).astype(jnp.float32)
    leads = lead > 0.5
    lead_edge = jnp.stack(lead_edge[::-1]).astype(jnp.float32)

    def orient(layers, row_two):
        parts = []
        for axis in range(2):
            layer = along(layers[axis], lane_one[axis], 1)
            layer = along(layer, row_two[axis], 0)
            parts.append(along(layer, lane_three[axis], 1))
        return jnp.stack(parts)

    cross_row, cross_lane = crossed(row_out[0]), crossed(lane_three[0])

    loads[4].wait()
    state = [nodes[k] for k in range(5)]
    velocity, pressure, warm = primitives(state)
    lifted = jnp.stack(velocity + [warm])
    own_velocity = [to_faces(v) for v in velocity]
    own_warm = to_faces(warm)
    own_lifted = own_velocity + [own_warm]
    loads[5].wait()
    metric = [[metv[g, d] for d in range(3)] for g in range(2)]
    own_row = [
        jnp.stack([to_faces(metric[0][d])[0], to_faces(metric[1][d])[1]]) for d in range(3)
    ]
    shown = own_lifted + [lead * own_row[d] for d in range(3)]
    shown = [[along(v[axis], lane_one[axis], 1) for axis in range(2)] for v in shown]
    for k in range(7):
        edge[0, k] = along(along(shown[k][0], cross_row, 0), cross_lane, 1)
        edge[1, k] = along(along(shown[k][1], row_out[1], 0), lane_three[1], 1)

    corner_sends = []
    for n, way in enumerate(diagonals):
        at = (3 if way[0] > 0 else 0) + (4 if way[1] > 0 else 0)
        corner_sends.append(
            pltpu.make_async_remote_copy(
                src_ref=edge.at[:, :, pl.ds(at, 1)],
                dst_ref=corner.at[:, :, pl.ds(7 - at, 1)],
                send_sem=ssem.at[4 + n],
                recv_sem=rsem.at[4 + n],
                device_id=target(way),
                device_id_type=MESH,
            )
        )
    corner_sends[0].start()
    corner_sends[2].start()
    seen = [
        jnp.stack([along(along(v[0], row_out[0], 0), lane_three[0], 1), edge[1, k]])
        for k, v in enumerate(shown)
    ]

    def products(g):
        return (lifted[:, None] * jnp.stack(metric[g])[None]).reshape(12, 2, 8, 128)

    loads[6].wait()
    loads[7].wait()
    metric.append([metv[2, d] for d in range(3)])
    partial = d_x(products(0)) + d_z(products(1)) + d_y(products(2))
    y_normal = [along(metric[2][d], y_lead, 1) for d in range(3)]
    y_sums = [
        y_side * (lifted[k] + (wall_sign if k < 3 else 1.0) * along(lifted[k], y_other, 1))
        for k in range(4)
    ]
    inverse_j = 1.0 / jacv[...]
    scaled = visc_coef * inverse_j
    partial = [
        [scaled * (partial[3 * k + d] + y_sums[k] * y_normal[d]) for d in range(3)]
        for k in range(4)
    ]
    face_partial = [[to_faces(partial[k][d]) for d in range(3)] for k in range(4)]
    face_scaled = to_faces(scaled)
    own = [to_faces(state[k]) for k in range(5)]
    for k in range(5):
        face[:, k] = own[k]
    for d in range(3):
        face[:, 5 + d] = own_row[d]
    for k in range(4):
        for d in range(3):
            face[:, 8 + 3 * k + d] = face_partial[k][d]
    face[:, 20] = face_scaled
    for d in range(3):
        across = to_faces(metric[1][d])[0], to_faces(metric[0][d])[1]
        face[:, 21 + d] = lead_edge * jnp.stack(across)

    sends = []
    for n, way in enumerate(sides):
        axis, from_up = n // 2, n % 2 == 0
        sends.append(
            pltpu.make_async_remote_copy(
                src_ref=face.at[axis, :, up if from_up else low],
                dst_ref=recv.at[axis, :, low if from_up else up],
                send_sem=ssem.at[n],
                recv_sem=rsem.at[n],
                device_id=target(way),
                device_id_type=MESH,
            )
        )
    sends[2].start()

    @pl.when(even)
    def _():
        sends[0].start()
        sends[1].start()

    pl.semaphore_wait(ready, 3)
    corner_sends[1].start()
    corner_sends[3].start()
    sends[3].start()

    @pl.when(jnp.logical_not(even))
    def _():
        sends[0].start()
        sends[1].start()

    inviscid = flows(state, velocity, pressure)
    own_inviscid = flows(own, own_velocity, to_faces(pressure))
    own_sound = jnp.sqrt(gamma_gas * own_warm)
    size_y = jnp.sqrt(dot3(y_normal, y_normal))
    speed = wave(velocity, jnp.sqrt(gamma_gas * warm), y_normal, size_y)
    speed = y_jump * jnp.maximum(speed, along(speed, y_other, 1))
    y_terms = []
    for k in range(5):
        sign = wall_sign if 1 <= k <= 3 else 1.0
        y_terms.append(speed * (state[k] - sign * along(state[k], y_other, 1)))
    mass_y = dot3(state[1:4], y_normal)
    mass_terms = y_terms[0] + y_side * (mass_y + wall_sign * along(mass_y, y_other, 1))
    mass_flux = [dot3(state[1:4], metric[g])[None] for g in range(3)]
    mass_terms = mass_terms + (d_x(mass_flux[0]) + d_z(mass_flux[1]) + d_y(mass_flux[2]))[0]
    mass_terms = -inverse_j * mass_terms

    for copy in sends:
        copy.wait_recv()

    they = [recv[:, k] for k in range(8)]
    they_scaled = recv[:, 20]
    they_velocity, they_pressure, they_warm = primitives(they)
    they_lifted = they_velocity + [they_warm]
    they_normal = [jnp.where(leads, seen[4 + d], they[5 + d]) for d in range(3)]
    they_sums = [(-3.0 * side) * (they_lifted[k] + seen[k]) for k in range(4)]
    they_slopes = [
        [
            recv[:, 8 + 3 * k + d]
            + (they_scaled * they_sums[k]) * they_normal[d]
            for d in range(3)
        ]
        for k in range(4)
    ]
    they_inviscid = flows(they, they_velocity, they_pressure)
    moment, energy = fluxes(they_inviscid, they_velocity, they_slopes)
    they_half = [dot3(they[1:4], they_normal)]
    they_half += [dot3(moment[j], they_normal) for j in range(3)]
    they_half += [dot3(energy, they_normal)]
    they_size = jnp.sqrt(dot3(they_normal, they_normal))
    they_speed = wave(they_velocity, jnp.sqrt(gamma_gas * they_warm), they_normal, they_size)

    other = [orient(they[k], row_in) for k in range(5)]
    other_half = [orient(they_half[k], row_in) for k in range(5)]
    other_speed = orient(they_speed, row_in)
    sums = [-orient(they_sums[k], row_in) for k in range(4)]
    normal = [jnp.where(leads, own_row[d], orient(they[5 + d], row_in)) for d in range(3)]

    def both_crossed(f):
        return jnp.stack([crossed(f[1]), crossed(f[0])])

    cross_sums = [z_edge * both_crossed(sums[k]) for k in range(4)]
    cross_normal = [both_crossed(normal[d]) for d in range(3)]
    face_slopes = [
        [
            face_partial[k][d]
            + face_scaled * (sums[k] * normal[d] + cross_sums[k] * cross_normal[d])
            for d in range(3)
        ]
        for k in range(4)
    ]
    moment, energy = fluxes(own_inviscid, own_velocity, face_slopes)
    own_half = [dot3(own[1:4], normal)]
    own_half += [dot3(moment[j], normal) for j in range(3)] + [dot3(energy, normal)]
    own_speed = wave(own_velocity, own_sound, normal, jnp.sqrt(dot3(normal, normal)))
    speed = 3.0 * jnp.maximum(own_speed, other_speed)
    tile_terms = [
        (3.0 * side) * (own_half[k] + other_half[k]) - speed * (other[k] - own[k])
        for k in range(5)
    ]

    z_sums = [jnp.stack([along(sums[k][1], z_index, 0), along(sums[k][1], z_index + 2, 0)]) * z_edge for k in range(4)]
    z_normal = [jnp.stack([along(normal[d][1], z_index, 0), along(normal[d][1], z_index + 2, 0)]) for d in range(3)]
    x_mask = jnp.stack(x_node)
    slopes = [
        [
            partial[k][d]
            + scaled * (x_mask * (sums[k][0] * normal[d][0]) + z_sums[k] * z_normal[d])
            for d in range(3)
        ]
        for k in range(4)
    ]
    moment, energy = fluxes(inviscid, velocity, slopes)

    def through(rows):
        return [dot3(moment[j], rows) for j in range(3)] + [dot3(energy, rows)]

    total = d_x(jnp.stack(through(metric[0])))
    total = total + d_z(jnp.stack(through(metric[1])))
    total = total + d_y(jnp.stack(through(metric[2])))

    half_y = through(y_normal)
    heat_y = (-2.0 * heat_ratio) * dot3(slopes[3], y_normal)
    for k in range(4):
        both = half_y[k] + along(half_y[k], y_other, 1)
        if k == 3:
            both = jnp.where(wall, heat_y, both)
        y_terms[1 + k] = y_terms[1 + k] + y_side * both
    out[0] = mass_terms - inverse_j * to_nodes(tile_terms[0])
    ready = [
        -inverse_j * (total[k] + y_terms[1 + k] + to_nodes(tile_terms[1 + k])) for k in range(4)
    ]

    for copy in corner_sends:
        copy.wait_recv()
    line = [jnp.stack([crossed(corner[1, k]), corner[0, k]]) for k in range(7)]
    line_sums = [
        (edge_side * they_scaled) * (they_lifted[k] + line[k]) for k in range(4)
    ]
    line_normal = [recv[:, 21 + d] + line[4 + d] for d in range(3)]
    onto = dot3(line_normal, they_normal)
    carried = dot3(line_sums, they_normal)
    spread = (2.0 / 3.0) * dot3(line_sums, line_normal)
    drag = [
        spread * they_normal[j] - line_sums[j] * onto - line_normal[j] * carried
        for j in range(3)
    ]
    drag.append(dot3(they_velocity, drag) - heat_ratio * (line_sums[3] * onto))
    for k in range(4):
        late = (3.0 * side) * orient(drag[k], row_in)
        out[1 + k] = ready[k] - inverse_j * to_nodes(late)
    for copy in sends + corner_sends:
        copy.wait_send()


def local(nx, nz, conserved, jacobian, metric, x_master, x_flip, z_master, z_flip):
    anywhere = pl.BlockSpec(memory_space=pl.ANY)
    words = [v.reshape(2, 32) for v in (x_master, x_flip, z_master, z_flip)]
    result = pl.pallas_call(
        functools.partial(kernel, nx, nz),
        out_shape=pltpu.VMEM((5, 2, 8, 128), jnp.float32),
        in_specs=[anywhere] * 7,
        out_specs=pl.BlockSpec(memory_space=pltpu.VMEM),
        scratch_shapes=[
            pltpu.VMEM((5, 2, 8, 128), jnp.float32),
            pltpu.VMEM((3, 3, 2, 8, 128), jnp.float32),
            pltpu.VMEM((2, 8, 128), jnp.float32),
            pltpu.VMEM((2, 24, 8, 128), jnp.float32),
            pltpu.VMEM((2, 24, 8, 128), jnp.float32),
            pltpu.VMEM((2, 7, 8, 128), jnp.float32),
            pltpu.VMEM((2, 7, 8, 128), jnp.float32),
            pltpu.VMEM((4, 2, 32), jnp.int32),
            pltpu.SemaphoreType.DMA((8,)),
            pltpu.SemaphoreType.DMA((8,)),
            pltpu.SemaphoreType.DMA((8,)),
            pltpu.SemaphoreType.REGULAR,
        ],
        compiler_params=pltpu.CompilerParams(collective_id=0, has_side_effects=True),
    )(
        conserved.reshape(5, 2, 8, 128),
        metric.reshape(3, 3, 2, 8, 128),
        jacobian.reshape(2, 8, 128),
        *words,
    )
    return result.reshape(5, 4, 4, 128)


def solution(mesh):
    flags = P("gx", "gz", None)
    in_specs = (P(None, "gx", "gz", None), flags, P(None, None, "gx", "gz", None)) + (flags,) * 4
    return jax.shard_map(
        functools.partial(local, mesh.shape["gx"], mesh.shape["gz"]),
        mesh=mesh,
        in_specs=in_specs,
        out_specs=P(None, "gx", "gz", None),
        check_vma=False,
    )
```
